32 devices in a mesh: ctx: 8 (over z, x), head: 4 (over y, core).
Axes of the slice: x: 2, y: 2, z: 4, core: 2. Of those that a mesh axis runs over, the one named last changes fastest.
Arguments:
- queries: bfloat16 [1024, 32, 576], P('ctx', 'head'), may hold values from -62 to 62
- latents: bfloat16 [1024, 576], P('ctx'), may hold values from -8 to 8
- out_grad: bfloat16 [1024, 32, 512], P('ctx', 'head'), may hold values from -6 to 6
- outputs: bfloat16 [1024, 32, 512], P('ctx', 'head'), may hold values from -4 to 4
- span_map: int32 [16], replicated, may hold values from 0 to 15, each once
Outputs:
- query_grads: bfloat16 [1024, 32, 576], P('ctx', 'head')
- latent_grads: float32 [1024, 576], P(('ctx', 'head'))
The draws below stay inside these ranges and needn't reach their ends.
Inputs may be any that keep to these rules, and one draw needn't show every extreme that they name: Stored span c holds the 64 tokens whose positions begin at span_map[c] * 64; every value appears once.
All inputs are finite; a program needn't handle non-finite values.
Results may differ from the reference program's by a relative error of at most 0.005.
Values may be sent and summed in bfloat16 or wider, within the bound.
No kernel may reach another device: no remote copies, remote signals or barrier semaphores. Data moves between devices by JAX's collectives and lax.ppermute only.
A program may use at most 64 MiB of HBM per device.

```python
import jax
import jax.numpy as jnp
from jax import lax

LATENT = 512
ROPE = 64
QK_HEAD = 192
HEADS = 32
KVW = 576
TOKENS = 1024
SPANS = 16


def draw_queries(key, part):
    key = jax.random.fold_in(key, 1)
    values = jax.random.truncated_normal(key, -4.0, 4.0, (TOKENS, HEADS, KVW), jnp.float32)
    return values.astype(jnp.bfloat16)


def draw_latents(key, part):
    key = jax.random.fold_in(key, 2)
    values = jax.random.truncated_normal(key, -4.0, 4.0, (TOKENS, KVW), jnp.float32)
    return values.astype(jnp.bfloat16)


def block_scale(stream_key, shape, pieces, smallest, largest):
    gain, own = 1.0, jax.random.fold_in(stream_key, 6)
    for dim, shards_of in pieces:
        steps = jnp.exp(jax.random.uniform(jax.random.fold_in(own, dim), (shards_of,), jnp.float32, smallest / len(pieces), largest / len(pieces)))
        gain = gain * jnp.repeat(steps, shape[dim] // shards_of).reshape([-1 if axis == dim else 1 for axis in range(len(shape))])
    return gain


def gaussian(stream_key, dims, deviation, reach, cuts=(), kind=jnp.bfloat16):
    array = jax.random.normal(stream_key, dims, jnp.float32) * deviation
    if len(cuts) > 0:
        array = block_scale(stream_key, dims, cuts, -0.22, 0.18) * array
    return jnp.clip(array, min=-reach, max=reach).astype(kind)


def setup_inputs(seed: int = 0) -> dict:
    keys = jax.random.split(jax.random.key(seed), 6)
    queries = draw_queries(jax.random.fold_in(keys[5], 71), 0)
    latents = draw_latents(jax.random.fold_in(keys[5], 71), 0)
    out_grad = gaussian(keys[2], (TOKENS, HEADS, LATENT), 1.0, 6.0, ((0, 8), (1, 4)))
    outputs = gaussian(keys[3], (TOKENS, HEADS, LATENT), 0.25, 4.0, ((0, 8), (1, 4)))
    span_map = jax.random.permutation(keys[4], SPANS).astype(jnp.int32)
    return dict(queries=queries, latents=latents, out_grad=out_grad, outputs=outputs, span_map=span_map)


LARGE_NEGATIVE = -1.0e30


def token_positions(span_map):
    span_rows = TOKENS // SPANS
    row_index = jnp.arange(TOKENS, dtype=jnp.int32)
    return (span_map[row_index // span_rows] * span_rows + row_index % span_rows).astype(jnp.int32)


def reference(queries, latents, out_grad, outputs, span_map):
    score_scale = QK_HEAD ** -0.5
    position = token_positions(span_map)
    allowed = position[None, :] <= position[:, None]

    def per_head(latent_sum, slices):
        query_rows, grad_rows, out_rows = slices
        scores = jnp.dot(query_rows, latents.T, preferred_element_type=jnp.float32) * score_scale
        highest = jnp.max(jnp.where(allowed, scores, LARGE_NEGATIVE), axis=1, keepdims=True)
        mass = jnp.sum(jnp.where(allowed, jnp.exp(scores - highest), 0.0), axis=1, keepdims=True)
        log_totals = highest + jnp.log(mass)
        weights = jnp.where(allowed, jnp.exp(scores - log_totals), 0.0)
        rounded = weights.astype(jnp.bfloat16)
        value_grads = jnp.dot(grad_rows, latents[:, :LATENT].T, preferred_element_type=jnp.float32)
        row_dots = jnp.sum(grad_rows.astype(jnp.float32) * out_rows.astype(jnp.float32), axis=1, keepdims=True)
        score_grads = (score_scale * weights * (value_grads - row_dots)).astype(jnp.bfloat16)
        query_grads = jnp.dot(score_grads, latents, preferred_element_type=jnp.float32).astype(jnp.bfloat16)
        key_part = jnp.dot(score_grads.T, query_rows, preferred_element_type=jnp.float32)
        value_part = jnp.dot(rounded.T, grad_rows, preferred_element_type=jnp.float32)
        latent_sum = latent_sum + key_part + jnp.pad(value_part, ((0, 0), (0, ROPE)))
        return latent_sum, query_grads

    slices = (jnp.transpose(queries, (1, 0, 2)), jnp.transpose(out_grad, (1, 0, 2)), jnp.transpose(outputs, (1, 0, 2)))
    latent_sum, query_grads = lax.scan(per_head, jnp.zeros((TOKENS, KVW), jnp.float32), slices)
    return jnp.transpose(query_grads, (1, 0, 2)), latent_sum
```

```python
import jax
import jax.numpy as jnp
from jax import lax
from jax.experimental import pallas as pl
from jax.experimental.pallas import tpu as pltpu
from jax.sharding import PartitionSpec as P

QK_HEAD = 192
LARGE_NEGATIVE = -1e30
LOG2_E = 1.4426950408889634
LANES = 128
VMEM_LIMIT = 40 * 1024 * 1024

f32 = jnp.float32
bf16 = jnp.bfloat16
VMEM = pl.BlockSpec(memory_space=pltpu.VMEM)


def dot(a, b, a_dim, b_dim):
    return lax.dot_general(a, b, (((a_dim,), (b_dim,)), ((), ())), preferred_element_type=f32)


def side_by_side(blocks):
    return jnp.concatenate(blocks, axis=1)


def latent_rows(ds_ref, p_ref, qt, out_grad, rows):
    key_term = dot(ds_ref[rows, :], qt, 1, 1)
    value_term = dot(p_ref[rows, :], out_grad, 1, 0)
    width = value_term.shape[1]
    return key_term[:, :width] + value_term, key_term[:, width:]


def probs_kernel(qt_ref, og_ref, rd_ref, k_ref, kpos_ref, qpos_ref, p_ref, ds_ref, far_ref):
    heads, _, tokens = qt_ref.shape
    width = og_ref.shape[2]
    keys = k_ref.shape[0]
    scale = QK_HEAD**-0.5
    group = 2
    for g in range(0, heads, group):
        some = range(g, g + group)
        cols = slice(g * tokens, (g + group) * tokens)
        qt = side_by_side([qt_ref[h] for h in some])
        scores = dot(k_ref[...], qt, 1, 0)
        allowed = side_by_side([kpos_ref[...]] * group) <= side_by_side([qpos_ref[...]] * group)
        scores = jnp.where(allowed, scores * (scale * LOG2_E), LARGE_NEGATIVE)
        mass = jnp.exp2(scores - jnp.max(scores, axis=0, keepdims=True))
        weights = mass * (1.0 / jnp.sum(mass, axis=0, keepdims=True))
        out_grad = og_ref[g : g + group].reshape(group * tokens, width)
        value_grads = dot(k_ref[:, :width], out_grad, 1, 1)
        row_dots = side_by_side([rd_ref[h] for h in some])
        p_ref[:, cols] = weights.astype(bf16)
        ds_ref[:, cols] = (weights * ((value_grads - row_dots) * scale)).astype(bf16)
    qt = side_by_side([qt_ref[h] for h in range(heads)])
    out_grad = og_ref[...].reshape(heads * tokens, width)
    half = keys // 2
    for r in range(0, half, 256):
        left, right = latent_rows(ds_ref, p_ref, qt, out_grad, slice(half + r, half + r + 256))
        far_ref[r : r + 256, :width] = left.astype(bf16)
        far_ref[r : r + 256, width:] = right.astype(bf16)


def near_kernel(qt_ref, og_ref, p_ref, ds_ref, near_ref):
    heads, _, tokens = qt_ref.shape
    width = og_ref.shape[2]
    qt = side_by_side([qt_ref[h] for h in range(heads)])
    out_grad = og_ref[...].reshape(heads * tokens, width)
    for r in range(0, near_ref.shape[0], 256):
        left, right = latent_rows(ds_ref, p_ref, qt, out_grad, slice(r, r + 256))
        near_ref[r : r + 256, :width] = left
        near_ref[r : r + 256, width:] = right


def query_kernel(k_ref, ds_ref, dq_ref):
    heads, _, tokens = dq_ref.shape
    for g in range(0, heads, 2):
        grads = dot(k_ref[...], ds_ref[:, g * tokens : (g + 2) * tokens], 0, 0).astype(bf16)
        dq_ref[g] = grads[:, :tokens]
        dq_ref[g + 1] = grads[:, tokens:]


def call(kernel, outs, flops, operands):
    return pl.pallas_call(
        kernel,
        in_specs=[VMEM] * len(operands),
        out_specs=[VMEM] * len(outs),
        out_shape=outs,
        compiler_params=pltpu.CompilerParams(vmem_limit_bytes=VMEM_LIMIT),
        cost_estimate=pl.CostEstimate(flops=flops, bytes_accessed=4 << 20, transcendentals=0),
    )(*operands)


def phases_of(device_count):
    bits = device_count.bit_length() - 1
    phases, bit = [[1]], 1
    while bit < bits:
        pair = [1 << bit] if bit + 1 == bits else [1 << bit, 2 << bit, 3 << bit]
        phases.append(pair)
        bit += len(pair).bit_length()
    return phases


def shards(queries, latents, out_grad, outputs, span_map):
    tokens, heads, kv_width = queries.shape
    width = out_grad.shape[2]
    head_size = lax.axis_size("head")
    devices = lax.axis_size("ctx") * head_size
    keys = lax.axis_size("ctx") * tokens
    span_rows = keys // span_map.shape[0]
    ctx, head = lax.axis_index("ctx"), lax.axis_index("head")
    me = ctx * head_size + head
    piece = tokens // head_size
    phases = phases_of(devices)

    def exchange(value, mask):
        return lax.ppermute(
            value, ("ctx", "head"), [(i, i ^ mask) for i in range(devices)]
        )

    def positions(rows):
        spans = rows // span_rows
        mine = spans[:, None] == jnp.arange(span_map.shape[0], dtype=jnp.int32)[None, :]
        return jnp.sum(jnp.where(mine, span_map[None, :], 0), axis=1) * span_rows + rows % span_rows

    order = [0]
    for masks in reversed(phases):
        order = order + [m ^ o for m in masks for o in order]
    starts = (me ^ jnp.array(order, dtype=jnp.int32)) * piece
    key_rows = (starts[:, None] + jnp.arange(piece, dtype=jnp.int32)[None, :]).reshape(-1)
    key_pos = jnp.broadcast_to(positions(key_rows)[:, None], (keys, LANES))
    query_pos = positions(ctx * tokens + jnp.arange(tokens, dtype=jnp.int32))[None, :]

    gathered = lax.dynamic_slice_in_dim(latents, head * piece, piece)
    for masks in reversed(phases):
        gathered = jnp.concatenate([gathered] + [exchange(gathered, m) for m in masks])

    qt = queries.transpose(1, 2, 0)
    og = out_grad.transpose(1, 0, 2)
    row_dots = jnp.einsum("ihc,ihc->hi", out_grad, outputs, preferred_element_type=f32)
    row_dots = row_dots.reshape(heads, 1, tokens)
    rows = heads * tokens
    half = keys // 2

    weights, score_grads, far = call(
        probs_kernel,
        [
            pltpu.VMEM((keys, rows), bf16),
            pltpu.VMEM((keys, rows), bf16),
            jax.ShapeDtypeStruct((half, kv_width), bf16),
        ],
        2 * keys * rows * (kv_width + width) * 2,
        [qt, og, row_dots, gathered, key_pos, query_pos],
    )
    arrived = exchange(far, 1)
    (near,) = call(
        near_kernel,
        [jax.ShapeDtypeStruct((half, kv_width), f32)],
        2 * half * rows * (kv_width + width),
        [qt, og, weights, score_grads],
    )
    (query_grads,) = call(
        query_kernel,
        [jax.ShapeDtypeStruct((heads, kv_width, tokens), bf16)],
        2 * keys * rows * kv_width,
        [gathered, score_grads],
    )
    total = near + arrived.astype(f32)
    for masks in phases[1:]:
        size = total.shape[0] // (len(masks) + 1)
        sent = total.astype(bf16)
        parts = [exchange(sent[(j + 1) * size : (j + 2) * size], m) for j, m in enumerate(masks)]
        total = total[:size] + sum(part.astype(f32) for part in parts)
    return query_grads.transpose(2, 0, 1), total


def solution(mesh):
    placed = (
        P("ctx", "head", None),
        P("ctx", None),
        P("ctx", "head", None),
        P("ctx", "head", None),
        P(),
    )
    return jax.shard_map(
        shards,
        mesh=mesh,
        in_specs=placed,
        out_specs=(P("ctx", "head", None), P(("ctx", "head"), None)),
        check_vma=False,
    )
```

```python
import jax
import jax.numpy as jnp
from jax import lax
from jax.experimental import pallas as pl
from jax.experimental.pallas import tpu as pltpu
from jax.sharding import PartitionSpec as P

QK_HEAD = 192
LARGE_NEGATIVE = -1e30
LOG2_E = 1.4426950408889634
LANES = 128
VMEM_LIMIT = 16 * 1024 * 1024

f32 = jnp.float32
bf16 = jnp.bfloat16
VMEM = pl.BlockSpec(memory_space=pltpu.VMEM)


def dot(a, b, a_dim, b_dim):
    return lax.dot_general(a, b, (((a_dim,), (b_dim,)), ((), ())), preferred_element_type=f32)


def side_by_side(blocks):
    return jnp.concatenate(blocks, axis=1)


def latent_rows(ds_ref, p_ref, qt, out_grad, rows):
    key_term = dot(ds_ref[rows, :], qt, 1, 1)
    value_term = dot(p_ref[rows, :], out_grad, 1, 0)
    width = value_term.shape[1]
    return key_term[:, :width] + value_term, key_term[:, width:]


def store_rows(out_ref, rows, left, right):
    width, used = left.shape[1], left.shape[1] + right.shape[1]
    out_ref[rows, :width] = left.astype(out_ref.dtype)
    out_ref[rows, width:used] = right.astype(out_ref.dtype)
    out_ref[rows, used:] = jnp.zeros((right.shape[0], out_ref.shape[1] - used), out_ref.dtype)


def latent_sums(out_ref, ds_ref, p_ref, qt, out_grad, first):
    step = min(256, out_ref.shape[0])
    for r in range(0, out_ref.shape[0], step):
        rows = slice(first + r, first + r + step)
        store_rows(out_ref, slice(r, r + step), *latent_rows(ds_ref, p_ref, qt, out_grad, rows))


GROUP = 2


def group_terms(qt_ref, og_ref, keys, kpos_ref, qpos_ref, g):
    _, kv_width, tokens = qt_ref.shape
    width = og_ref.shape[2]
    qt = side_by_side([qt_ref[h] for h in range(g, g + GROUP)])
    scores = dot(keys[:, :kv_width], qt, 1, 0)
    allowed = side_by_side([kpos_ref[...]] * GROUP) <= side_by_side([qpos_ref[...]] * GROUP)
    scores = jnp.where(allowed, scores * (QK_HEAD**-0.5 * LOG2_E), LARGE_NEGATIVE)
    out_grad = og_ref[g : g + GROUP].reshape(GROUP * tokens, width)
    return scores, dot(keys[:, :width], out_grad, 1, 1)


def stacked(refs):
    return jnp.concatenate([ref[...] for ref in refs])


def partial_kernel(qt_ref, og_ref, kpos_ref, qpos_ref, *refs):
    *piece_refs, mass_ref, vg_ref, peak_ref, sum_ref = refs
    heads, _, tokens = qt_ref.shape
    keys = stacked(piece_refs)
    for g in range(0, heads, GROUP):
        cols = slice(g * tokens, (g + GROUP) * tokens)
        scores, vg_ref[:, cols] = group_terms(qt_ref, og_ref, keys, kpos_ref, qpos_ref, g)
        peak = jnp.max(scores, axis=0, keepdims=True)
        mass = jnp.exp2(scores - peak)
        mass_ref[:, cols] = mass
        peak_ref[:, cols] = peak
        sum_ref[:, cols] = jnp.sum(mass, axis=0, keepdims=True)


def probs_kernel(qt_ref, og_ref, rd_ref, kpos_ref, qpos_ref, *refs):
    *refs, p_ref, ds_ref, far_ref = refs
    *piece_refs, mass0, vg0, peak0, sum0, mass1, vg1, peak1, sum1 = refs
    heads, _, tokens = qt_ref.shape
    width = og_ref.shape[2]
    half = p_ref.shape[0] // 2
    own = mass0.shape[0] // 2
    scale = QK_HEAD**-0.5
    keys = stacked(piece_refs)
    for g in range(0, heads, GROUP):
        cols = slice(g * tokens, (g + GROUP) * tokens)
        scores, grads = group_terms(qt_ref, og_ref, keys, kpos_ref, qpos_ref, g)
        last = jnp.max(scores, axis=0, keepdims=True)
        peak = jnp.maximum(jnp.maximum(peak0[:, cols], peak1[:, cols]), last)
        mass = jnp.exp2(scores - peak)
        ratio0, ratio1 = jnp.exp2(peak0[:, cols] - peak), jnp.exp2(peak1[:, cols] - peak)
        total = sum0[:, cols] * ratio0 + sum1[:, cols] * ratio1 + jnp.sum(mass, axis=0, keepdims=True)
        inverse = 1.0 / total
        row_dots = side_by_side([rd_ref[h] for h in range(g, g + GROUP)])
        parts = (
            (slice(0, own), mass0[:own, cols], vg0[:own, cols], inverse * ratio0),
            (slice(half, half + own), mass0[own:, cols], vg0[own:, cols], inverse * ratio0),
            (slice(own, half), mass1[:, cols], vg1[:, cols], inverse * ratio1),
            (slice(half + own, 2 * half), mass, grads, inverse),
        )
        for rows, part, value_grads, factor in parts:
            weights = part * factor
            p_ref[rows, cols] = weights.astype(bf16)
            ds_ref[rows, cols] = (weights * ((value_grads - row_dots) * scale)).astype(bf16)
    qt = side_by_side([qt_ref[h] for h in range(heads)])
    out_grad = og_ref[...].reshape(heads * tokens, width)
    latent_sums(far_ref, ds_ref, p_ref, qt, out_grad, half)


def first_kernel(qt_ref, og_ref, p_ref, ds_ref, near_ref, far_ref):
    heads, _, tokens = qt_ref.shape
    half = p_ref.shape[0] // 2
    qt = side_by_side([qt_ref[h] for h in range(heads)])
    out_grad = og_ref[...].reshape(heads * tokens, og_ref.shape[2])
    latent_sums(near_ref, ds_ref, p_ref, qt, out_grad, 0)
    latent_sums(far_ref, ds_ref, p_ref, qt, out_grad, half + half // 2)


def last_kernel(qt_ref, og_ref, p_ref, ds_ref, after_ref, near_ref):
    heads, _, tokens = qt_ref.shape
    half = p_ref.shape[0] // 2
    qt = side_by_side([qt_ref[h] for h in range(heads)])
    out_grad = og_ref[...].reshape(heads * tokens, og_ref.shape[2])
    latent_sums(near_ref, ds_ref, p_ref, qt, out_grad, half // 2)


def query_kernel(ds_ref, *refs):
    *piece_refs, dq_ref = refs
    heads, kv_width, tokens = dq_ref.shape
    keys = stacked(piece_refs)[:, :kv_width]
    for g in range(0, heads, GROUP):
        grads = dot(keys, ds_ref[:, g * tokens : (g + GROUP) * tokens], 0, 0).astype(bf16)
        for i in range(GROUP):
            dq_ref[g + i] = grads[:, i * tokens : (i + 1) * tokens]


def call(kernel, outs, flops, operands):
    return list(pl.pallas_call(
        kernel,
        in_specs=[VMEM] * len(operands),
        out_specs=[VMEM] * len(outs),
        out_shape=outs,
        compiler_params=pltpu.CompilerParams(vmem_limit_bytes=VMEM_LIMIT),
        cost_estimate=pl.CostEstimate(flops=flops, bytes_accessed=4 << 20, transcendentals=0),
    )(*operands))


def phases_of(device_count):
    bits = device_count.bit_length() - 1
    phases, bit = [[1]], 1
    while bit < bits:
        pair = [1 << bit] if bit + 1 == bits else [1 << bit, 2 << bit, 3 << bit]
        phases.append(pair)
        bit += 1 if len(pair) == 1 else 2
    return phases


def shards(queries, latents, out_grad, outputs, span_map):
    tokens, heads, kv_width = queries.shape
    width = out_grad.shape[2]
    head_size = lax.axis_size("head")
    devices = lax.axis_size("ctx") * head_size
    keys = lax.axis_size("ctx") * tokens
    span_rows = keys // span_map.shape[0]
    ctx, head = lax.axis_index("ctx"), lax.axis_index("head")
    me = ctx * head_size + head
    piece = tokens // head_size
    phases = phases_of(devices)
    around = phases[1][-1:] + phases[1][:-1]
    half_order = [0]
    for masks in [*reversed(phases[2:]), around]:
        half_order = half_order + [m ^ o for m in masks for o in half_order]

    def exchange(value, mask):
        return lax.ppermute(
            value, ("ctx", "head"), [(i, i ^ mask) for i in range(devices)]
        )

    def positions(spans, rows):
        at = rows // span_rows
        mine = at[:, None] == jnp.arange(spans.shape[0], dtype=jnp.int32)[None, :]
        return jnp.sum(jnp.where(mine, spans[None, :], 0), axis=1) * span_rows + rows % span_rows

    qt = queries.transpose(1, 2, 0)
    rows = heads * tokens
    half = keys // 2
    padded = -(-kv_width // LANES) * LANES
    pair_macs = half * rows * (kv_width + width)

    own = lax.dynamic_slice_in_dim(latents, head * piece, piece)
    own = jnp.pad(own, ((0, 0), (0, padded - kv_width)))
    for masks in reversed(phases[2:]):
        own = jnp.concatenate([own] + [exchange(own, m) for m in masks])
    own, out_grad, outputs, span_map = lax.optimization_barrier((own, out_grad, outputs, span_map))
    near = {m: exchange(own, m) for m in phases[1]}
    near = [near[m] for m in around]
    og = out_grad.transpose(1, 0, 2)
    row_dots = jnp.einsum("ihc,ihc->hi", out_grad, outputs, preferred_element_type=f32)
    row_dots = row_dots.reshape(heads, 1, tokens)
    starts = (me ^ jnp.array(half_order, dtype=jnp.int32)) * piece
    near_rows = (starts[:, None] + jnp.arange(piece, dtype=jnp.int32)[None, :]).reshape(-1)
    near_pos = positions(span_map, near_rows)
    far_pos = positions(span_map, near_rows + jnp.where(head % 2 == 0, piece, -piece))
    query_pos = positions(span_map, ctx * tokens + jnp.arange(tokens, dtype=jnp.int32))[None, :]
    owned = own.shape[0]
    own, row_dots = lax.optimization_barrier((own, row_dots))
    own_far = exchange(own, 1)

    def in_lanes(pos):
        return jnp.broadcast_to(pos[:, None], (pos.shape[0], LANES))

    def partial_terms(pos, pieces):
        count = sum(p.shape[0] for p in pieces)
        return call(
            partial_kernel,
            [
                pltpu.VMEM((count, rows), f32),
                pltpu.VMEM((count, rows), f32),
                pltpu.VMEM((1, rows), f32),
                pltpu.VMEM((1, rows), f32),
            ],
            2 * count * rows * (kv_width + width),
            [qt, og, pos, query_pos, *pieces],
        )

    own_lanes, near_lanes, far_lanes = lax.optimization_barrier(
        (
            in_lanes(jnp.concatenate([near_pos[:owned], far_pos[:owned]])),
            in_lanes(near_pos[owned:]),
            in_lanes(far_pos[owned:]),
        )
    )
    terms0 = partial_terms(own_lanes, [own, own_far])
    near, terms0[2] = lax.optimization_barrier((near, terms0[2]))
    far = [exchange(p, 1) for p in near]
    terms1 = partial_terms(near_lanes, near)
    weights, score_grads, far_a = call(
        probs_kernel,
        [
            pltpu.VMEM((keys, rows), bf16),
            pltpu.VMEM((keys, rows), bf16),
            jax.ShapeDtypeStruct((half // 2, padded), bf16),
        ],
        3 * pair_macs,
        [qt, og, row_dots, far_lanes, query_pos, *far, *terms0, *terms1],
    )
    arrived = exchange(far_a, 1)
    near_a, far_b = call(
        first_kernel,
        [
            jax.ShapeDtypeStruct((half // 2, padded), f32),
            jax.ShapeDtypeStruct((half // 2, padded), bf16),
        ],
        2 * pair_macs,
        [qt, og, weights, score_grads],
    )
    size = half // (len(around) + 1)
    kept = near_a + arrived.astype(f32)
    leading, after = lax.optimization_barrier((kept[size:].astype(bf16), terms0[2]))
    parts = [exchange(leading, around[0])]
    kept = kept[:size]
    arrived = exchange(far_b, 1)
    (near_b,) = call(
        last_kernel,
        [jax.ShapeDtypeStruct((half // 2, padded), f32)],
        pair_macs,
        [qt, og, weights, score_grads, after],
    )
    if len(around) > 1:
        sent = (near_b + arrived.astype(f32)).astype(bf16)
        parts += [exchange(sent[j * size : (j + 1) * size], m) for j, m in enumerate(around[1:])]
    total = kept + sum(part.astype(f32) for part in parts)
    (query_grads,) = call(
        query_kernel,
        [jax.ShapeDtypeStruct((heads, kv_width, tokens), bf16)],
        4 * half * rows * kv_width,
        [score_grads, own, *near, own_far, *far],
    )
    total, query_grads = lax.optimization_barrier((total, query_grads))
    for masks in phases[2:]:
        size = total.shape[0] // (len(masks) + 1)
        sent = total.astype(bf16)
        parts = {j: sent[(j + 1) * size : (j + 2) * size] for j in range(len(masks))}
        far_first = [len(masks) - 1, *range(len(masks) - 1)]
        total = total[:size] + sum(exchange(parts[j], masks[j]).astype(f32) for j in far_first)
    return query_grads.transpose(2, 0, 1), total[:, :kv_width]


def solution(mesh):
    placed = (
        P("ctx", "head", None),
        P("ctx", None),
        P("ctx", "head", None),
        P("ctx", "head", None),
        P(),
    )
    return jax.shard_map(
        shards,
        mesh=mesh,
        in_specs=placed,
        out_specs=(P("ctx", "head", None), P(("ctx", "head"), None)),
        check_vma=False,
    )
```

```python
import functools

import jax
import jax.numpy as jnp
from jax import lax
from jax.experimental import pallas as pl
from jax.experimental.pallas import tpu as pltpu
from jax.sharding import PartitionSpec as P

QK_HEAD = 192
LARGE_NEGATIVE = -1e30
LOG2_E = 1.4426950408889634
LANES = 128
VMEM_LIMIT = 8 * 1024 * 1024

f32 = jnp.float32
bf16 = jnp.bfloat16
VMEM = pl.BlockSpec(memory_space=pltpu.VMEM)


def dot(a, b, a_dim, b_dim):
    return lax.dot_general(a, b, (((a_dim,), (b_dim,)), ((), ())), preferred_element_type=f32)


def side_by_side(blocks):
    return jnp.concatenate(blocks, axis=1)


def latent_rows(ds_ref, p_ref, qt, out_grad, rows):
    key_term = dot(ds_ref[rows, :], qt, 1, 1)
    value_term = dot(p_ref[rows, :], out_grad, 1, 0)
    width = value_term.shape[1]
    return key_term[:, :width] + value_term, key_term[:, width:]


def packed(rows):
    count, width = rows.shape
    whole = width // LANES * LANES
    blocks = [rows[:, c : c + LANES] for c in range(0, whole, LANES)]
    if whole < width:
        rest = rows[:, whole:]
        blocks.append(jnp.concatenate([rest[: count // 2], rest[count // 2 :]], axis=1))
    return jnp.concatenate(blocks)


def unpacked(blocks, count, width):
    whole = width // LANES
    columns = [blocks[c * count : (c + 1) * count] for c in range(whole)]
    if whole * LANES < width:
        rest = blocks[whole * count :]
        half = LANES // 2
        columns.append(jnp.concatenate([rest[:, :half], rest[:, half:]]))
    return jnp.concatenate(columns, axis=1)


def stored_pieces(out_ref, first, piece, left, right):
    width, rest = left.shape[1], right.shape[1]
    if not piece:
        rows = slice(first, first + left.shape[0])
        out_ref[rows, :width] = left.astype(out_ref.dtype)
        out_ref[rows, width : width + rest] = right.astype(out_ref.dtype)
        unused = out_ref.shape[1] - width - rest
        out_ref[rows, width + rest :] = jnp.zeros((left.shape[0], unused), out_ref.dtype)
        return
    high = piece * (width + rest) // LANES
    for r in range(0, left.shape[0], piece):
        base = (first + r) // piece * high
        for c in range(0, width, LANES):
            at = base + c // LANES * piece
            out_ref[at : at + piece, :] = left[r : r + piece, c : c + LANES].astype(out_ref.dtype)
        middle = r + piece // 2
        folded = jnp.concatenate([right[r:middle], right[middle : r + piece]], axis=1)
        out_ref[base + width // LANES * piece : base + high, :] = folded.astype(out_ref.dtype)


def key_rows(refs, piece, kv_width):
    if not piece:
        return jnp.concatenate([ref[:, :kv_width] for ref in refs])
    high = piece * kv_width // LANES
    return jnp.concatenate(
        [
            unpacked(ref[r : r + high, :], piece, kv_width)
            for ref in refs
            for r in range(0, ref.shape[0], high)
        ]
    )


def latent_sums(out_ref, piece, count, ds_ref, p_ref, qt, out_grad, first):
    step = min(256, count)
    for r in range(0, count, step):
        rows = slice(first + r, first + r + step)
        stored_pieces(out_ref, r, piece, *latent_rows(ds_ref, p_ref, qt, out_grad, rows))


GROUP = 2


def group_terms(qt_ref, og_ref, keys, kpos_ref, qpos_ref, g):
    tokens = qt_ref.shape[2]
    width = og_ref.shape[2]
    qt = side_by_side([qt_ref[h] for h in range(g, g + GROUP)])
    scores = dot(keys, qt, 1, 0)
    allowed = side_by_side([kpos_ref[...]] * GROUP) <= side_by_side([qpos_ref[...]] * GROUP)
    scores = jnp.where(allowed, scores * (QK_HEAD**-0.5 * LOG2_E), LARGE_NEGATIVE)
    out_grad = og_ref[g : g + GROUP].reshape(GROUP * tokens, width)
    return scores, dot(keys[:, :width], out_grad, 1, 1)


def pack_kernel(piece, rows_ref, out_ref):
    out_ref[...] = packed(rows_ref[...])


def partial_kernel(piece, qt_ref, og_ref, kpos_ref, qpos_ref, *refs):
    *piece_refs, mass_ref, vg_ref, peak_ref, sum_ref = refs
    heads, _, tokens = qt_ref.shape
    keys = key_rows(piece_refs, piece, qt_ref.shape[1])
    for g in range(0, heads, GROUP):
        cols = slice(g * tokens, (g + GROUP) * tokens)
        scores, vg_ref[:, cols] = group_terms(qt_ref, og_ref, keys, kpos_ref, qpos_ref, g)
        peak = jnp.max(scores, axis=0, keepdims=True)
        mass = jnp.exp2(scores - peak)
        mass_ref[:, cols] = mass
        peak_ref[:, cols] = peak
        sum_ref[:, cols] = jnp.sum(mass, axis=0, keepdims=True)


def probs_kernel(piece, qt_ref, og_ref, rd_ref, kpos_ref, qpos_ref, *refs):
    *refs, p_ref, ds_ref, far_ref = refs
    *piece_refs, mass0, vg0, peak0, sum0, mass1, vg1, peak1, sum1 = refs
    heads, _, tokens = qt_ref.shape
    width = og_ref.shape[2]
    half = p_ref.shape[0] // 2
    own = mass0.shape[0] // 2
    scale = QK_HEAD**-0.5
    keys = key_rows(piece_refs, piece, qt_ref.shape[1])
    for g in range(0, heads, GROUP):
        cols = slice(g * tokens, (g + GROUP) * tokens)
        scores, grads = group_terms(qt_ref, og_ref, keys, kpos_ref, qpos_ref, g)
        last = jnp.max(scores, axis=0, keepdims=True)
        peak = jnp.maximum(jnp.maximum(peak0[:, cols], peak1[:, cols]), last)
        mass = jnp.exp2(scores - peak)
        ratio0, ratio1 = jnp.exp2(peak0[:, cols] - peak), jnp.exp2(peak1[:, cols] - peak)
        total = sum0[:, cols] * ratio0 + sum1[:, cols] * ratio1 + jnp.sum(mass, axis=0, keepdims=True)
        inverse = 1.0 / total
        row_dots = side_by_side([rd_ref[h] for h in range(g, g + GROUP)])
        parts = (
            (slice(0, own), mass0[:own, cols], vg0[:own, cols], inverse * ratio0),
            (slice(half, half + own), mass0[own:, cols], vg0[own:, cols], inverse * ratio0),
            (slice(own, half), mass1[:, cols], vg1[:, cols], inverse * ratio1),
            (slice(half + own, 2 * half), mass, grads, inverse),
        )
        for rows, part, value_grads, factor in parts:
            weights = part * factor
            p_ref[rows, cols] = weights.astype(bf16)
            ds_ref[rows, cols] = (weights * ((value_grads - row_dots) * scale)).astype(bf16)
    qt = side_by_side([qt_ref[h] for h in range(heads)])
    out_grad = og_ref[...].reshape(heads * tokens, width)
    latent_sums(far_ref, piece, half // 2, ds_ref, p_ref, qt, out_grad, half)


def first_kernel(piece, qt_ref, og_ref, p_ref, ds_ref, near_ref, far_ref):
    heads, _, tokens = qt_ref.shape
    half = p_ref.shape[0] // 2
    qt = side_by_side([qt_ref[h] for h in range(heads)])
    out_grad = og_ref[...].reshape(heads * tokens, og_ref.shape[2])
    latent_sums(near_ref, piece, half // 2, ds_ref, p_ref, qt, out_grad, 0)
    latent_sums(far_ref, piece, half // 2, ds_ref, p_ref, qt, out_grad, half + half // 2)


def last_kernel(piece, qt_ref, og_ref, p_ref, ds_ref, after_ref, near_ref):
    heads, _, tokens = qt_ref.shape
    half = p_ref.shape[0] // 2
    qt = side_by_side([qt_ref[h] for h in range(heads)])
    out_grad = og_ref[...].reshape(heads * tokens, og_ref.shape[2])
    latent_sums(near_ref, piece, half // 2, ds_ref, p_ref, qt, out_grad, half // 2)


def query_kernel(piece, ds_ref, *refs):
    *piece_refs, dq_ref = refs
    heads, kv_width, tokens = dq_ref.shape
    keys = key_rows(piece_refs, piece, kv_width)
    for g in range(0, heads, GROUP):
        grads = dot(keys, ds_ref[:, g * tokens : (g + GROUP) * tokens], 0, 0).astype(bf16)
        for i in range(GROUP):
            dq_ref[g + i] = grads[:, i * tokens : (i + 1) * tokens]


def call(kernel, outs, flops, operands):
    return list(pl.pallas_call(
        kernel,
        in_specs=[VMEM] * len(operands),
        out_specs=[VMEM] * len(outs),
        out_shape=outs,
        compiler_params=pltpu.CompilerParams(vmem_limit_bytes=VMEM_LIMIT),
        cost_estimate=pl.CostEstimate(flops=flops, bytes_accessed=4 << 20, transcendentals=0),
    )(*operands))


def phases_of(device_count):
    bits = device_count.bit_length() - 1
    phases, bit = [[1]], 1
    while bit < bits:
        pair = [1 << bit] if bit + 1 == bits else [1 << bit, 2 << bit, 3 << bit]
        phases.append(pair)
        bit += 1 if len(pair) == 1 else 2
    return phases


def shards(queries, latents, out_grad, outputs, span_map):
    tokens, heads, kv_width = queries.shape
    width = out_grad.shape[2]
    head_size = lax.axis_size("head")
    devices = lax.axis_size("ctx") * head_size
    keys = lax.axis_size("ctx") * tokens
    span_rows = keys // span_map.shape[0]
    ctx, head = lax.axis_index("ctx"), lax.axis_index("head")
    me = ctx * head_size + head
    piece = tokens // head_size
    phases = phases_of(devices)
    around = phases[1][-1:] + phases[1][:-1]
    half_order = [0]
    for masks in [*reversed(phases[2:]), around]:
        half_order = half_order + [m ^ o for m in masks for o in half_order]

    def exchange(value, mask):
        return lax.ppermute(
            value, ("ctx", "head"), [(i, i ^ mask) for i in range(devices)]
        )

    def positions(spans, rows):
        at = rows // span_rows
        mine = at[:, None] == jnp.arange(spans.shape[0], dtype=jnp.int32)[None, :]
        return jnp.sum(jnp.where(mine, spans[None, :], 0), axis=1) * span_rows + rows % span_rows

    qt = queries.transpose(1, 2, 0)
    rows = heads * tokens
    half = keys // 2
    unit = piece if piece % 32 == 0 and kv_width % LANES == LANES // 2 else 0
    columns = LANES if unit else -(-kv_width // LANES) * LANES

    def high(count):
        return count * kv_width // LANES if unit else count

    def kernel(body):
        return functools.partial(body, unit)

    pair_macs = half * rows * (kv_width + width)

    own = lax.dynamic_slice_in_dim(latents, head * piece, piece)
    if unit:
        packed_shape = jax.ShapeDtypeStruct((high(piece), LANES), bf16)
        (own,) = call(kernel(pack_kernel), [packed_shape], 0, [own])
    else:
        own = jnp.pad(own, ((0, 0), (0, columns - kv_width)))
    for masks in reversed(phases[2:]):
        own = jnp.concatenate([own] + [exchange(own, m) for m in masks])
    own, out_grad, outputs, span_map = lax.optimization_barrier((own, out_grad, outputs, span_map))
    near = {m: exchange(own, m) for m in phases[1]}
    near = [near[m] for m in around]
    og = out_grad.transpose(1, 0, 2)
    row_dots = jnp.einsum("ihc,ihc->hi", out_grad, outputs, preferred_element_type=f32)
    row_dots = row_dots.reshape(heads, 1, tokens)
    starts = (me ^ jnp.array(half_order, dtype=jnp.int32)) * piece
    near_rows = (starts[:, None] + jnp.arange(piece, dtype=jnp.int32)[None, :]).reshape(-1)
    near_pos = positions(span_map, near_rows)
    far_pos = positions(span_map, near_rows + jnp.where(head % 2 == 0, piece, -piece))
    query_pos = positions(span_map, ctx * tokens + jnp.arange(tokens, dtype=jnp.int32))[None, :]
    owned = half // (len(around) + 1)
    own, row_dots = lax.optimization_barrier((own, row_dots))
    own_far = exchange(own, 1)

    def in_lanes(pos):
        return jnp.broadcast_to(pos[:, None], (pos.shape[0], LANES))

    def partial_terms(pos, pieces):
        count = pos.shape[0]
        return call(
            kernel(partial_kernel),
            [
                pltpu.VMEM((count, rows), f32),
                pltpu.VMEM((count, rows), f32),
                pltpu.VMEM((1, rows), f32),
                pltpu.VMEM((1, rows), f32),
            ],
            2 * count * rows * (kv_width + width),
            [qt, og, pos, query_pos, *pieces],
        )

    own_lanes, near_lanes, far_lanes = lax.optimization_barrier(
        (
            in_lanes(jnp.concatenate([near_pos[:owned], far_pos[:owned]])),
            in_lanes(near_pos[owned:]),
            in_lanes(far_pos[owned:]),
        )
    )
    terms0 = partial_terms(own_lanes, [own, own_far])
    near, terms0[2] = lax.optimization_barrier((near, terms0[2]))
    far = [exchange(p, 1) for p in near]
    terms1 = partial_terms(near_lanes, near)
    weights, score_grads, far_a = call(
        kernel(probs_kernel),
        [
            pltpu.VMEM((keys, rows), bf16),
            pltpu.VMEM((keys, rows), bf16),
            jax.ShapeDtypeStruct((high(half // 2), columns), bf16),
        ],
        3 * pair_macs,
        [qt, og, row_dots, far_lanes, query_pos, *far, *terms0, *terms1],
    )
    arrived = exchange(far_a, 1)
    near_a, far_b = call(
        kernel(first_kernel),
        [
            jax.ShapeDtypeStruct((high(half // 2), columns), f32),
            jax.ShapeDtypeStruct((high(half // 2), columns), bf16),
        ],
        2 * pair_macs,
        [qt, og, weights, score_grads],
    )
    size = high(owned)
    kept = near_a + arrived.astype(f32)
    leading, after = lax.optimization_barrier((kept[size:].astype(bf16), terms0[2]))
    parts = [exchange(leading, around[0])]
    kept = kept[:size]
    arrived = exchange(far_b, 1)
    (near_b,) = call(
        kernel(last_kernel),
        [jax.ShapeDtypeStruct((high(half // 2), columns), f32)],
        pair_macs,
        [qt, og, weights, score_grads, after],
    )
    if len(around) > 1:
        sent = (near_b + arrived.astype(f32)).astype(bf16)
        parts += [exchange(sent[j * size : (j + 1) * size], m) for j, m in enumerate(around[1:])]
    total = kept + sum(part.astype(f32) for part in parts)
    (query_grads,) = call(
        kernel(query_kernel),
        [jax.ShapeDtypeStruct((heads, kv_width, tokens), bf16)],
        4 * half * rows * kv_width,
        [score_grads, own, *near, own_far, *far],
    )
    total, query_grads = lax.optimization_barrier((total, query_grads))
    for masks in phases[2:]:
        size = total.shape[0] // (len(masks) + 1)
        sent = total.astype(bf16)
        parts = {j: sent[(j + 1) * size : (j + 2) * size] for j in range(len(masks))}
        far_first = [len(masks) - 1, *range(len(masks) - 1)]
        total = total[:size] + sum(exchange(parts[j], masks[j]).astype(f32) for j in far_first)
    latent_grads = unpacked(total, piece, kv_width) if unit else total[:, :kv_width]
    return query_grads.transpose(2, 0, 1), latent_grads


def solution(mesh):
    placed = (
        P("ctx", "head", None),
        P("ctx", None),
        P("ctx", "head", None),
        P("ctx", "head", None),
        P(),
    )
    return jax.shard_map(
        shards,
        mesh=mesh,
        in_specs=placed,
        out_specs=(P("ctx", "head", None), P(("ctx", "head"), None)),
        check_vma=False,
    )
```

```python
import functools

import jax
import jax.numpy as jnp
from jax import lax
from jax.experimental import pallas as pl
from jax.experimental.pallas import tpu as pltpu
from jax.sharding import PartitionSpec as P

QK_HEAD = 192
LARGE_NEGATIVE = -1e30
LOG2_E = 1.4426950408889634
LANES = 128
VMEM_LIMIT = 8 * 1024 * 1024

f32 = jnp.float32
bf16 = jnp.bfloat16
VMEM = pl.BlockSpec(memory_space=pltpu.VMEM)


def dot(a, b, a_dim, b_dim):
    return lax.dot_general(a, b, (((a_dim,), (b_dim,)), ((), ())), preferred_element_type=f32)


def side_by_side(blocks):
    return jnp.concatenate(blocks, axis=1)


def latent_rows(ds_ref, p_ref, qt, out_grad, rows):
    key_term = dot(ds_ref[rows, :], qt, 1, 1)
    value_term = dot(p_ref[rows, :], out_grad, 1, 0)
    width = value_term.shape[1]
    return key_term[:, :width] + value_term, key_term[:, width:]


def packed(rows):
    count, width = rows.shape
    whole = width // LANES * LANES
    blocks = [rows[:, c : c + LANES] for c in range(0, whole, LANES)]
    if whole < width:
        rest = rows[:, whole:]
        blocks.append(jnp.concatenate([rest[: count // 2], rest[count // 2 :]], axis=1))
    return jnp.concatenate(blocks)


def unpacked(blocks, count, width):
    whole = width // LANES
    columns = [blocks[c * count : (c + 1) * count] for c in range(whole)]
    if whole * LANES < width:
        rest = blocks[whole * count :]
        half = LANES // 2
        columns.append(jnp.concatenate([rest[:, :half], rest[:, half:]]))
    return jnp.concatenate(columns, axis=1)


def stored_pieces(out_ref, first, piece, left, right):
    width, rest = left.shape[1], right.shape[1]
    if not piece:
        rows = slice(first, first + left.shape[0])
        out_ref[rows, :width] = left.astype(out_ref.dtype)
        out_ref[rows, width : width + rest] = right.astype(out_ref.dtype)
        unused = out_ref.shape[1] - width - rest
        out_ref[rows, width + rest :] = jnp.zeros((left.shape[0], unused), out_ref.dtype)
        return
    high = piece * (width + rest) // LANES
    for r in range(0, left.shape[0], piece):
        base = (first + r) // piece * high
        for c in range(0, width, LANES):
            at = base + c // LANES * piece
            out_ref[at : at + piece, :] = left[r : r + piece, c : c + LANES].astype(out_ref.dtype)
        middle = r + piece // 2
        folded = jnp.concatenate([right[r:middle], right[middle : r + piece]], axis=1)
        out_ref[base + width // LANES * piece : base + high, :] = folded.astype(out_ref.dtype)


def key_rows(refs, piece, kv_width):
    if not piece:
        return jnp.concatenate([ref[:, :kv_width] for ref in refs])
    high = piece * kv_width // LANES
    return jnp.concatenate(
        [
            unpacked(ref[r : r + high, :], piece, kv_width)
            for ref in refs
            for r in range(0, ref.shape[0], high)
        ]
    )


def latent_sums(out_ref, piece, count, ds_ref, p_ref, qt, out_grad, first):
    step = min(256, count)
    for r in range(0, count, step):
        rows = slice(first + r, first + r + step)
        stored_pieces(out_ref, r, piece, *latent_rows(ds_ref, p_ref, qt, out_grad, rows))


GROUP = 4


def group_terms(qt_ref, og_ref, keys, kpos_ref, qpos_ref, g):
    tokens = qt_ref.shape[2]
    width = og_ref.shape[2]
    qt = side_by_side([qt_ref[h] for h in range(g, g + GROUP)])
    scores = dot(keys, qt, 1, 0)
    allowed = side_by_side([kpos_ref[...]] * GROUP) <= side_by_side([qpos_ref[...]] * GROUP)
    scores = jnp.where(allowed, scores * (QK_HEAD**-0.5 * LOG2_E), LARGE_NEGATIVE)
    out_grad = og_ref[g : g + GROUP].reshape(GROUP * tokens, width)
    return scores, dot(keys[:, :width], out_grad, 1, 1)


def pack_kernel(piece, rows_ref, out_ref):
    out_ref[...] = packed(rows_ref[...])


def partial_kernel(piece, qt_ref, og_ref, kpos_ref, qpos_ref, *refs):
    *piece_refs, mass_ref, vg_ref, peak_ref, sum_ref = refs
    heads, _, tokens = qt_ref.shape
    keys = key_rows(piece_refs, piece, qt_ref.shape[1])
    for g in range(0, heads, GROUP):
        cols = slice(g * tokens, (g + GROUP) * tokens)
        scores, vg_ref[:, cols] = group_terms(qt_ref, og_ref, keys, kpos_ref, qpos_ref, g)
        peak = jnp.max(scores, axis=0, keepdims=True)
        mass = jnp.exp2(scores - peak)
        mass_ref[:, cols] = mass
        peak_ref[:, cols] = peak
        sum_ref[:, cols] = jnp.sum(mass, axis=0, keepdims=True)


def probs_kernel(piece, qt_ref, og_ref, rd_ref, kpos_ref, qpos_ref, *refs):
    *refs, p_ref, ds_ref, far_ref = refs
    *piece_refs, mass0, vg0, peak0, sum0, mass1, vg1, peak1, sum1 = refs
    heads, _, tokens = qt_ref.shape
    width = og_ref.shape[2]
    half = p_ref.shape[0] // 2
    own = mass0.shape[0] // 2
    scale = QK_HEAD**-0.5
    keys = key_rows(piece_refs, piece, qt_ref.shape[1])
    for g in range(0, heads, GROUP):
        cols = slice(g * tokens, (g + GROUP) * tokens)
        scores, grads = group_terms(qt_ref, og_ref, keys, kpos_ref, qpos_ref, g)
        last = jnp.max(scores, axis=0, keepdims=True)
        peak = jnp.maximum(jnp.maximum(peak0[:, cols], peak1[:, cols]), last)
        mass = jnp.exp2(scores - peak)
        ratio0, ratio1 = jnp.exp2(peak0[:, cols] - peak), jnp.exp2(peak1[:, cols] - peak)
        total = sum0[:, cols] * ratio0 + sum1[:, cols] * ratio1 + jnp.sum(mass, axis=0, keepdims=True)
        inverse = 1.0 / total
        row_dots = side_by_side([rd_ref[h] for h in range(g, g + GROUP)])
        parts = (
            (slice(0, own), mass0[:own, cols], vg0[:own, cols], inverse * ratio0),
            (slice(half, half + own), mass0[own:, cols], vg0[own:, cols], inverse * ratio0),
            (slice(own, half), mass1[:, cols], vg1[:, cols], inverse * ratio1),
            (slice(half + own, 2 * half), mass, grads, inverse),
        )
        for rows, part, value_grads, factor in parts:
            weights = part * factor
            p_ref[rows, cols] = weights.astype(bf16)
            ds_ref[rows, cols] = (weights * ((value_grads - row_dots) * scale)).astype(bf16)
    qt = side_by_side([qt_ref[h] for h in range(heads)])
    out_grad = og_ref[...].reshape(heads * tokens, width)
    latent_sums(far_ref, piece, half // 2, ds_ref, p_ref, qt, out_grad, half)


def first_kernel(piece, qt_ref, og_ref, p_ref, ds_ref, near_ref, far_ref):
    heads, _, tokens = qt_ref.shape
    half = p_ref.shape[0] // 2
    qt = side_by_side([qt_ref[h] for h in range(heads)])
    out_grad = og_ref[...].reshape(heads * tokens, og_ref.shape[2])
    latent_sums(near_ref, piece, half // 2, ds_ref, p_ref, qt, out_grad, 0)
    latent_sums(far_ref, piece, half // 2, ds_ref, p_ref, qt, out_grad, half + half // 2)


def last_kernel(piece, qt_ref, og_ref, p_ref, ds_ref, after_ref, near_ref):
    heads, _, tokens = qt_ref.shape
    half = p_ref.shape[0] // 2
    qt = side_by_side([qt_ref[h] for h in range(heads)])
    out_grad = og_ref[...].reshape(heads * tokens, og_ref.shape[2])
    latent_sums(near_ref, piece, half // 2, ds_ref, p_ref, qt, out_grad, half // 2)


def query_kernel(piece, ds_ref, *refs):
    *piece_refs, dq_ref = refs
    heads, kv_width, tokens = dq_ref.shape
    keys = key_rows(piece_refs, piece, kv_width)
    for g in range(0, heads, GROUP):
        grads = dot(keys, ds_ref[:, g * tokens : (g + GROUP) * tokens], 0, 0).astype(bf16)
        for i in range(GROUP):
            dq_ref[g + i] = grads[:, i * tokens : (i + 1) * tokens]


def call(kernel, outs, flops, operands):
    return list(pl.pallas_call(
        kernel,
        in_specs=[VMEM] * len(operands),
        out_specs=[VMEM] * len(outs),
        out_shape=outs,
        compiler_params=pltpu.CompilerParams(vmem_limit_bytes=VMEM_LIMIT),
        cost_estimate=pl.CostEstimate(flops=flops, bytes_accessed=4 << 20, transcendentals=0),
    )(*operands))


def phases_of(device_count):
    bits = device_count.bit_length() - 1
    phases, bit = [[1]], 1
    while bit < bits:
        pair = [1 << bit] if bit + 1 == bits else [1 << bit, 2 << bit, 3 << bit]
        phases.append(pair)
        bit += 1 if len(pair) == 1 else 2
    return phases


def shards(queries, latents, out_grad, outputs, span_map):
    tokens, heads, kv_width = queries.shape
    width = out_grad.shape[2]
    head_size = lax.axis_size("head")
    devices = lax.axis_size("ctx") * head_size
    keys = lax.axis_size("ctx") * tokens
    span_rows = keys // span_map.shape[0]
    ctx, head = lax.axis_index("ctx"), lax.axis_index("head")
    me = ctx * head_size + head
    piece = tokens // head_size
    phases = phases_of(devices)
    around = phases[1][-1:] + phases[1][:-1]
    half_order = [0]
    for masks in [*reversed(phases[2:]), around]:
        half_order = half_order + [m ^ o for m in masks for o in half_order]

    def exchange(value, mask):
        return lax.ppermute(
            value, ("ctx", "head"), [(i, i ^ mask) for i in range(devices)]
        )

    def positions(spans, rows):
        at = rows // span_rows
        mine = at[:, None] == jnp.arange(spans.shape[0], dtype=jnp.int32)[None, :]
        return jnp.sum(jnp.where(mine, spans[None, :], 0), axis=1) * span_rows + rows % span_rows

    qt = queries.transpose(1, 2, 0)
    rows = heads * tokens
    half = keys // 2
    unit = piece if piece % 32 == 0 and kv_width % LANES == LANES // 2 else 0
    columns = LANES if unit else -(-kv_width // LANES) * LANES

    def high(count):
        return count * kv_width // LANES if unit else count

    def kernel(body):
        return functools.partial(body, unit)

    pair_macs = half * rows * (kv_width + width)

    own = lax.dynamic_slice_in_dim(latents, head * piece, piece)
    if unit:
        packed_shape = jax.ShapeDtypeStruct((high(piece), LANES), bf16)
        (own,) = call(kernel(pack_kernel), [packed_shape], 0, [own])
    else:
        own = jnp.pad(own, ((0, 0), (0, columns - kv_width)))
    for masks in reversed(phases[2:]):
        own = jnp.concatenate([own] + [exchange(own, m) for m in masks])
    own, out_grad, outputs, span_map = lax.optimization_barrier((own, out_grad, outputs, span_map))
    near = {m: exchange(own, m) for m in phases[1]}
    near = [near[m] for m in around]
    og = out_grad.transpose(1, 0, 2)
    row_dots = jnp.einsum("ihc,ihc->hi", out_grad, outputs, preferred_element_type=f32)
    row_dots = row_dots.reshape(heads, 1, tokens)
    starts = (me ^ jnp.array(half_order, dtype=jnp.int32)) * piece
    near_rows = (starts[:, None] + jnp.arange(piece, dtype=jnp.int32)[None, :]).reshape(-1)
    near_pos = positions(span_map, near_rows)
    far_pos = positions(span_map, near_rows + jnp.where(head % 2 == 0, piece, -piece))
    query_pos = positions(span_map, ctx * tokens + jnp.arange(tokens, dtype=jnp.int32))[None, :]
    owned = half // (len(around) + 1)
    own, row_dots = lax.optimization_barrier((own, row_dots))
    own_far = exchange(own, 1)

    def in_lanes(pos):
        return jnp.broadcast_to(pos[:, None], (pos.shape[0], LANES))

    def partial_terms(pos, pieces):
        count = pos.shape[0]
        return call(
            kernel(partial_kernel),
            [
                pltpu.VMEM((count, rows), f32),
                pltpu.VMEM((count, rows), f32),
                pltpu.VMEM((1, rows), f32),
                pltpu.VMEM((1, rows), f32),
            ],
            2 * count * rows * (kv_width + width),
            [qt, og, pos, query_pos, *pieces],
        )

    own_lanes, near_lanes, far_lanes = lax.optimization_barrier(
        (
            in_lanes(jnp.concatenate([near_pos[:owned], far_pos[:owned]])),
            in_lanes(near_pos[owned:]),
            in_lanes(far_pos[owned:]),
        )
    )
    terms0 = partial_terms(own_lanes, [own, own_far])
    near, terms0[2] = lax.optimization_barrier((near, terms0[2]))
    far = [exchange(p, 1) for p in near]
    terms1 = partial_terms(near_lanes, near)
    weights, score_grads, far_a = call(
        kernel(probs_kernel),
        [
            pltpu.VMEM((keys, rows), bf16),
            pltpu.VMEM((keys, rows), bf16),
            jax.ShapeDtypeStruct((high(half // 2), columns), bf16),
        ],
        3 * pair_macs,
        [qt, og, row_dots, far_lanes, query_pos, *far, *terms0, *terms1],
    )
    arrived = exchange(far_a, 1)
    near_a, far_b = call(
        kernel(first_kernel),
        [
            jax.ShapeDtypeStruct((high(half // 2), columns), f32),
            jax.ShapeDtypeStruct((high(half // 2), columns), bf16),
        ],
        2 * pair_macs,
        [qt, og, weights, score_grads],
    )
    size = high(owned)
    kept = near_a + arrived.astype(f32)
    leading, after = lax.optimization_barrier((kept[size:].astype(bf16), terms0[2]))
    parts = [exchange(leading, around[0])]
    kept = kept[:size]
    arrived = exchange(far_b, 1)
    (near_b,) = call(
        kernel(last_kernel),
        [jax.ShapeDtypeStruct((high(half // 2), columns), f32)],
        pair_macs,
        [qt, og, weights, score_grads, after],
    )
    if len(around) > 1:
        sent = (near_b + arrived.astype(f32)).astype(bf16)
        parts += [exchange(sent[j * size : (j + 1) * size], m) for j, m in enumerate(around[1:])]
    total = kept + sum(part.astype(f32) for part in parts)
    (query_grads,) = call(
        kernel(query_kernel),
        [jax.ShapeDtypeStruct((heads, kv_width, tokens), bf16)],
        4 * half * rows * kv_width,
        [score_grads, own, *near, own_far, *far],
    )
    total, query_grads = lax.optimization_barrier((total, query_grads))
    for masks in phases[2:]:
        size = total.shape[0] // (len(masks) + 1)
        sent = total.astype(bf16)
        parts = {j: sent[(j + 1) * size : (j + 2) * size] for j in range(len(masks))}
        far_first = [len(masks) - 1, *range(len(masks) - 1)]
        total = total[:size] + sum(exchange(parts[j], masks[j]).astype(f32) for j in far_first)
    latent_grads = unpacked(total, piece, kv_width) if unit else total[:, :kv_width]
    return query_grads.transpose(2, 0, 1), latent_grads


def solution(mesh):
    placed = (
        P("ctx", "head", None),
        P("ctx", None),
        P("ctx", "head", None),
        P("ctx", "head", None),
        P(),
    )
    return jax.shard_map(
        shards,
        mesh=mesh,
        in_specs=placed,
        out_specs=(P("ctx", "head", None), P(("ctx", "head"), None)),
        check_vma=False,
    )
```

```python
import functools

import jax
import jax.numpy as jnp
from jax import lax
from jax.experimental import pallas as pl
from jax.experimental.pallas import tpu as pltpu
from jax.sharding import PartitionSpec as P

QK_HEAD = 192
LARGE_NEGATIVE = -1e30
LOG2_E = 1.4426950408889634
LANES = 128
VMEM_LIMIT = 8 * 1024 * 1024

f32 = jnp.float32
bf16 = jnp.bfloat16
VMEM = pl.BlockSpec(memory_space=pltpu.VMEM)


def dot(a, b, a_dim, b_dim):
    return lax.dot_general(a, b, (((a_dim,), (b_dim,)), ((), ())), preferred_element_type=f32)


def side_by_side(blocks):
    return jnp.concatenate(blocks, axis=1)


def latent_rows(ds_ref, p_ref, qt, out_grad, rows):
    key_term = dot(ds_ref[rows, :], qt, 1, 1)
    value_term = dot(p_ref[rows, :], out_grad, 1, 0)
    width = value_term.shape[1]
    return key_term[:, :width] + value_term, key_term[:, width:]


def packed(rows):
    count, width = rows.shape
    whole = width // LANES * LANES
    blocks = [rows[:, c : c + LANES] for c in range(0, whole, LANES)]
    if whole < width:
        rest = rows[:, whole:]
        blocks.append(jnp.concatenate([rest[: count // 2], rest[count // 2 :]], axis=1))
    return jnp.concatenate(blocks)


def unpacked(blocks, count, width):
    whole = width // LANES
    columns = [blocks[c * count : (c + 1) * count] for c in range(whole)]
    if whole * LANES < width:
        rest = blocks[whole * count :]
        half = LANES // 2
        columns.append(jnp.concatenate([rest[:, :half], rest[:, half:]]))
    return jnp.concatenate(columns, axis=1)


def stored_pieces(out_ref, first, piece, left, right):
    width, rest = left.shape[1], right.shape[1]
    if not piece:
        rows = slice(first, first + left.shape[0])
        out_ref[rows, :width] = left.astype(out_ref.dtype)
        out_ref[rows, width : width + rest] = right.astype(out_ref.dtype)
        unused = out_ref.shape[1] - width - rest
        out_ref[rows, width + rest :] = jnp.zeros((left.shape[0], unused), out_ref.dtype)
        return
    high = piece * (width + rest) // LANES
    for r in range(0, left.shape[0], piece):
        base = (first + r) // piece * high
        for c in range(0, width, LANES):
            at = base + c // LANES * piece
            out_ref[at : at + piece, :] = left[r : r + piece, c : c + LANES].astype(out_ref.dtype)
        middle = r + piece // 2
        folded = jnp.concatenate([right[r:middle], right[middle : r + piece]], axis=1)
        out_ref[base + width // LANES * piece : base + high, :] = folded.astype(out_ref.dtype)


def key_rows(refs, piece, kv_width):
    if not piece:
        return jnp.concatenate([ref[:, :kv_width] for ref in refs])
    high = piece * kv_width // LANES
    return jnp.concatenate(
        [
            unpacked(ref[r : r + high, :], piece, kv_width)
            for ref in refs
            for r in range(0, ref.shape[0], high)
        ]
    )


def latent_sums(out_ref, piece, count, ds_ref, p_ref, qt, out_grad, first):
    step = min(256, count)
    for r in range(0, count, step):
        rows = slice(first + r, first + r + step)
        stored_pieces(out_ref, r, piece, *latent_rows(ds_ref, p_ref, qt, out_grad, rows))


GROUP = 4


def group_terms(qt_ref, og_ref, keys, kpos_ref, qpos_ref, g):
    tokens = qt_ref.shape[2]
    width = og_ref.shape[2]
    qt = side_by_side([qt_ref[h] for h in range(g, g + GROUP)])
    scores = dot(keys, qt, 1, 0)
    allowed = side_by_side([kpos_ref[...]] * GROUP) <= side_by_side([qpos_ref[...]] * GROUP)
    scores = jnp.where(allowed, scores * (QK_HEAD**-0.5 * LOG2_E), LARGE_NEGATIVE)
    out_grad = og_ref[g : g + GROUP].reshape(GROUP * tokens, width)
    return scores, dot(keys[:, :width], out_grad, 1, 1)


def pack_kernel(piece, rows_ref, out_ref):
    out_ref[...] = packed(rows_ref[...])


def partial_kernel(piece, qt_ref, og_ref, rd_ref, kpos_ref, qpos_ref, *refs):
    *piece_refs, mass_ref, vg_ref, peak_ref, sum_ref = refs
    heads, _, tokens = qt_ref.shape
    keys = key_rows(piece_refs, piece, qt_ref.shape[1])
    for g in range(0, heads, GROUP):
        cols = slice(g * tokens, (g + GROUP) * tokens)
        scores, value_grads = group_terms(qt_ref, og_ref, keys, kpos_ref, qpos_ref, g)
        row_dots = side_by_side([rd_ref[h] for h in range(g, g + GROUP)])
        vg_ref[:, cols] = (value_grads - row_dots) * QK_HEAD**-0.5
        peak = jnp.max(scores, axis=0, keepdims=True)
        mass = jnp.exp2(scores - peak)
        mass_ref[:, cols] = mass
        peak_ref[:, cols] = peak
        sum_ref[:, cols] = jnp.sum(mass, axis=0, keepdims=True)


def probs_kernel(piece, qt_ref, og_ref, rd_ref, kpos_ref, qpos_ref, *refs):
    *refs, p_ref, ds_ref, far_ref = refs
    *piece_refs, mass0, vg0, peak0, sum0, mass1, vg1, peak1, sum1 = refs
    heads, _, tokens = qt_ref.shape
    width = og_ref.shape[2]
    half = p_ref.shape[0] // 2
    own = mass0.shape[0] // 2
    scale = QK_HEAD**-0.5
    keys = key_rows(piece_refs, piece, qt_ref.shape[1])
    for g in range(0, heads, GROUP):
        cols = slice(g * tokens, (g + GROUP) * tokens)
        scores, grads = group_terms(qt_ref, og_ref, keys, kpos_ref, qpos_ref, g)
        last = jnp.max(scores, axis=0, keepdims=True)
        peak = jnp.maximum(jnp.maximum(peak0[:, cols], peak1[:, cols]), last)
        mass = jnp.exp2(scores - peak)
        ratio0, ratio1 = jnp.exp2(peak0[:, cols] - peak), jnp.exp2(peak1[:, cols] - peak)
        total = sum0[:, cols] * ratio0 + sum1[:, cols] * ratio1 + jnp.sum(mass, axis=0, keepdims=True)
        inverse = 1.0 / total
        row_dots = side_by_side([rd_ref[h] for h in range(g, g + GROUP)])
        parts = (
            (slice(0, own), mass0[:own, cols], vg0[:own, cols], inverse * ratio0),
            (slice(half, half + own), mass0[own:, cols], vg0[own:, cols], inverse * ratio0),
            (slice(own, half), mass1[:, cols], vg1[:, cols], inverse * ratio1),
            (slice(half + own, 2 * half), mass, (grads - row_dots) * scale, inverse),
        )
        for rows, part, value_grads, factor in parts:
            weights = part * factor
            p_ref[rows, cols] = weights.astype(bf16)
            ds_ref[rows, cols] = (weights * value_grads).astype(bf16)
    qt = side_by_side([qt_ref[h] for h in range(heads)])
    out_grad = og_ref[...].reshape(heads * tokens, width)
    latent_sums(far_ref, piece, half // 2, ds_ref, p_ref, qt, out_grad, half)


def first_kernel(piece, qt_ref, og_ref, p_ref, ds_ref, near_ref, far_ref):
    heads, _, tokens = qt_ref.shape
    half = p_ref.shape[0] // 2
    qt = side_by_side([qt_ref[h] for h in range(heads)])
    out_grad = og_ref[...].reshape(heads * tokens, og_ref.shape[2])
    latent_sums(near_ref, piece, half // 2, ds_ref, p_ref, qt, out_grad, 0)
    latent_sums(far_ref, piece, half // 2, ds_ref, p_ref, qt, out_grad, half + half // 2)


def last_kernel(piece, qt_ref, og_ref, p_ref, ds_ref, after_ref, near_ref):
    heads, _, tokens = qt_ref.shape
    half = p_ref.shape[0] // 2
    qt = side_by_side([qt_ref[h] for h in range(heads)])
    out_grad = og_ref[...].reshape(heads * tokens, og_ref.shape[2])
    latent_sums(near_ref, piece, half // 2, ds_ref, p_ref, qt, out_grad, half // 2)


def query_kernel(piece, ds_ref, *refs):
    *piece_refs, dq_ref = refs
    heads, kv_width, tokens = dq_ref.shape
    keys = key_rows(piece_refs, piece, kv_width)
    for g in range(0, heads, GROUP):
        grads = dot(keys, ds_ref[:, g * tokens : (g + GROUP) * tokens], 0, 0).astype(bf16)
        for i in range(GROUP):
            dq_ref[g + i] = grads[:, i * tokens : (i + 1) * tokens]


def call(kernel, outs, flops, operands):
    return list(pl.pallas_call(
        kernel,
        in_specs=[VMEM] * len(operands),
        out_specs=[VMEM] * len(outs),
        out_shape=outs,
        compiler_params=pltpu.CompilerParams(vmem_limit_bytes=VMEM_LIMIT),
        cost_estimate=pl.CostEstimate(flops=flops, bytes_accessed=4 << 20, transcendentals=0),
    )(*operands))


def phases_of(device_count):
    bits = device_count.bit_length() - 1
    phases, bit = [[1]], 1
    while bit < bits:
        pair = [1 << bit] if bit + 1 == bits else [1 << bit, 2 << bit, 3 << bit]
        phases.append(pair)
        bit += 1 if len(pair) == 1 else 2
    return phases


def shards(queries, latents, out_grad, outputs, span_map):
    tokens, heads, kv_width = queries.shape
    width = out_grad.shape[2]
    head_size = lax.axis_size("head")
    devices = lax.axis_size("ctx") * head_size
    keys = lax.axis_size("ctx") * tokens
    span_rows = keys // span_map.shape[0]
    ctx, head = lax.axis_index("ctx"), lax.axis_index("head")
    me = ctx * head_size + head
    piece = tokens // head_size
    phases = phases_of(devices)
    around = phases[1][-1:] + phases[1][:-1]
    half_order = [0]
    for masks in [*reversed(phases[2:]), around]:
        half_order = half_order + [m ^ o for m in masks for o in half_order]

    def exchange(value, mask):
        return lax.ppermute(
            value, ("ctx", "head"), [(i, i ^ mask) for i in range(devices)]
        )

    def positions(spans, rows):
        at = rows // span_rows
        mine = at[:, None] == jnp.arange(spans.shape[0], dtype=jnp.int32)[None, :]
        return jnp.sum(jnp.where(mine, spans[None, :], 0), axis=1) * span_rows + rows % span_rows

    qt = queries.transpose(1, 2, 0)
    rows = heads * tokens
    half = keys // 2
    unit = piece if piece % 32 == 0 and kv_width % LANES == LANES // 2 else 0
    columns = LANES if unit else -(-kv_width // LANES) * LANES

    def high(count):
        return count * kv_width // LANES if unit else count

    def kernel(body):
        return functools.partial(body, unit)

    pair_macs = half * rows * (kv_width + width)

    own = lax.dynamic_slice_in_dim(latents, head * piece, piece)
    if unit:
        packed_shape = jax.ShapeDtypeStruct((high(piece), LANES), bf16)
        (own,) = call(kernel(pack_kernel), [packed_shape], 0, [own])
    else:
        own = jnp.pad(own, ((0, 0), (0, columns - kv_width)))
    for masks in reversed(phases[2:]):
        own = jnp.concatenate([own] + [exchange(own, m) for m in masks])
    own, out_grad, outputs, span_map = lax.optimization_barrier((own, out_grad, outputs, span_map))
    near = {m: exchange(own, m) for m in phases[1]}
    near = [near[m] for m in around]
    og = out_grad.transpose(1, 0, 2)
    row_dots = jnp.einsum("ihc,ihc->hi", out_grad, outputs, preferred_element_type=f32)
    row_dots = row_dots.reshape(heads, 1, tokens)
    starts = (me ^ jnp.array(half_order, dtype=jnp.int32)) * piece
    near_rows = (starts[:, None] + jnp.arange(piece, dtype=jnp.int32)[None, :]).reshape(-1)
    near_pos = positions(span_map, near_rows)
    far_pos = positions(span_map, near_rows + jnp.where(head % 2 == 0, piece, -piece))
    query_pos = positions(span_map, ctx * tokens + jnp.arange(tokens, dtype=jnp.int32))[None, :]
    owned = half // (len(around) + 1)
    own, row_dots = lax.optimization_barrier((own, row_dots))
    own_far = exchange(own, 1)

    def in_lanes(pos):
        return jnp.broadcast_to(pos[:, None], (pos.shape[0], LANES))

    def partial_terms(pos, pieces):
        count = pos.shape[0]
        return call(
            kernel(partial_kernel),
            [
                pltpu.VMEM((count, rows), f32),
                pltpu.VMEM((count, rows), f32),
                pltpu.VMEM((1, rows), f32),
                pltpu.VMEM((1, rows), f32),
            ],
            2 * count * rows * (kv_width + width),
            [qt, og, row_dots, pos, query_pos, *pieces],
        )

    own_lanes, near_lanes, far_lanes = lax.optimization_barrier(
        (
            in_lanes(jnp.concatenate([near_pos[:owned], far_pos[:owned]])),
            in_lanes(near_pos[owned:]),
            in_lanes(far_pos[owned:]),
        )
    )
    terms0 = partial_terms(own_lanes, [own, own_far])
    near, terms0[2] = lax.optimization_barrier((near, terms0[2]))
    far = [exchange(p, 1) for p in near]
    terms1 = partial_terms(near_lanes, near)
    weights, score_grads, far_a = call(
        kernel(probs_kernel),
        [
            pltpu.VMEM((keys, rows), bf16),
            pltpu.VMEM((keys, rows), bf16),
            jax.ShapeDtypeStruct((high(half // 2), columns), bf16),
        ],
        3 * pair_macs,
        [qt, og, row_dots, far_lanes, query_pos, *far, *terms0, *terms1],
    )
    arrived = exchange(far_a, 1)
    near_a, far_b = call(
        kernel(first_kernel),
        [
            jax.ShapeDtypeStruct((high(half // 2), columns), f32),
            jax.ShapeDtypeStruct((high(half // 2), columns), bf16),
        ],
        2 * pair_macs,
        [qt, og, weights, score_grads],
    )
    size = high(owned)
    kept = near_a + arrived.astype(f32)
    leading, after = lax.optimization_barrier((kept[size:].astype(bf16), terms0[2]))
    parts = [exchange(leading, around[0])]
    kept = kept[:size]
    arrived = exchange(far_b, 1)
    (near_b,) = call(
        kernel(last_kernel),
        [jax.ShapeDtypeStruct((high(half // 2), columns), f32)],
        pair_macs,
        [qt, og, weights, score_grads, after],
    )
    if len(around) > 1:
        sent = (near_b + arrived.astype(f32)).astype(bf16)
        parts += [exchange(sent[j * size : (j + 1) * size], m) for j, m in enumerate(around[1:])]
    total = kept + sum(part.astype(f32) for part in parts)
    (query_grads,) = call(
        kernel(query_kernel),
        [jax.ShapeDtypeStruct((heads, kv_width, tokens), bf16)],
        4 * half * rows * kv_width,
        [score_grads, own, *near, own_far, *far],
    )
    total, query_grads = lax.optimization_barrier((total, query_grads))
    for masks in phases[2:]:
        size = total.shape[0] // (len(masks) + 1)
        sent = total.astype(bf16)
        parts = {j: sent[(j + 1) * size : (j + 2) * size] for j in range(len(masks))}
        far_first = [len(masks) - 1, *range(len(masks) - 1)]
        total = total[:size] + sum(exchange(parts[j], masks[j]).astype(f32) for j in far_first)
    latent_grads = unpacked(total, piece, kv_width) if unit else total[:, :kv_width]
    return query_grads.transpose(2, 0, 1), latent_grads


def solution(mesh):
    placed = (
        P("ctx", "head", None),
        P("ctx", None),
        P("ctx", "head", None),
        P("ctx", "head", None),
        P(),
    )
    return jax.shard_map(
        shards,
        mesh=mesh,
        in_specs=placed,
        out_specs=(P("ctx", "head", None), P(("ctx", "head"), None)),
        check_vma=False,
    )
```

```python
import functools

import jax
import jax.numpy as jnp
from jax import lax
from jax.experimental import pallas as pl
from jax.experimental.pallas import tpu as pltpu
from jax.sharding import PartitionSpec as P

QK_HEAD = 192
LARGE_NEGATIVE = -1e30
LOG2_E = 1.4426950408889634
LANES = 128
VMEM_LIMIT = 8 * 1024 * 1024

f32 = jnp.float32
bf16 = jnp.bfloat16
VMEM = pl.BlockSpec(memory_space=pltpu.VMEM)


def dot(a, b, a_dim, b_dim):
    return lax.dot_general(a, b, (((a_dim,), (b_dim,)), ((), ())), preferred_element_type=f32)


def side_by_side(blocks):
    return jnp.concatenate(blocks, axis=1)


def latent_rows(ds_ref, p_ref, qt, out_grad, rows):
    key_term = dot(ds_ref[rows, :], qt, 1, 1)
    value_term = dot(p_ref[rows, :], out_grad, 1, 0)
    width = value_term.shape[1]
    return key_term[:, :width] + value_term, key_term[:, width:]


def packed(rows):
    count, width = rows.shape
    whole = width // LANES * LANES
    blocks = [rows[:, c : c + LANES] for c in range(0, whole, LANES)]
    if whole < width:
        rest = rows[:, whole:]
        blocks.append(jnp.concatenate([rest[: count // 2], rest[count // 2 :]], axis=1))
    return jnp.concatenate(blocks)


def unpacked(blocks, count, width):
    whole = width // LANES
    columns = [blocks[c * count : (c + 1) * count] for c in range(whole)]
    if whole * LANES < width:
        rest = blocks[whole * count :]
        half = LANES // 2
        columns.append(jnp.concatenate([rest[:, :half], rest[:, half:]]))
    return jnp.concatenate(columns, axis=1)


def stored_pieces(out_ref, first, piece, left, right):
    width, rest = left.shape[1], right.shape[1]
    if not piece:
        rows = slice(first, first + left.shape[0])
        out_ref[rows, :width] = left.astype(out_ref.dtype)
        out_ref[rows, width : width + rest] = right.astype(out_ref.dtype)
        unused = out_ref.shape[1] - width - rest
        out_ref[rows, width + rest :] = jnp.zeros((left.shape[0], unused), out_ref.dtype)
        return
    high = piece * (width + rest) // LANES
    for r in range(0, left.shape[0], piece):
        base = (first + r) // piece * high
        for c in range(0, width, LANES):
            at = base + c // LANES * piece
            out_ref[at : at + piece, :] = left[r : r + piece, c : c + LANES].astype(out_ref.dtype)
        middle = r + piece // 2
        folded = jnp.concatenate([right[r:middle], right[middle : r + piece]], axis=1)
        out_ref[base + width // LANES * piece : base + high, :] = folded.astype(out_ref.dtype)


def key_rows(refs, piece, kv_width):
    if not piece:
        return jnp.concatenate([ref[:, :kv_width] for ref in refs])
    high = piece * kv_width // LANES
    return jnp.concatenate(
        [
            unpacked(ref[r : r + high, :], piece, kv_width)
            for ref in refs
            for r in range(0, ref.shape[0], high)
        ]
    )


def latent_sums(out_ref, piece, count, ds_ref, p_ref, qt, out_grad, first):
    step = min(256, count)
    for r in range(0, count, step):
        rows = slice(first + r, first + r + step)
        stored_pieces(out_ref, r, piece, *latent_rows(ds_ref, p_ref, qt, out_grad, rows))


GROUP = 4


def group_terms(qt_ref, og_ref, keys, kpos, qpos_ref, g):
    tokens = qt_ref.shape[2]
    width = og_ref.shape[2]
    qt = side_by_side([qt_ref[h] for h in range(g, g + GROUP)])
    scores = dot(keys, qt, 1, 0)
    allowed = side_by_side([kpos] * GROUP) <= side_by_side([qpos_ref[...]] * GROUP)
    scores = jnp.where(allowed, scores * (QK_HEAD**-0.5 * LOG2_E), LARGE_NEGATIVE)
    out_grad = og_ref[g : g + GROUP].reshape(GROUP * tokens, width)
    return scores, dot(keys[:, :width], out_grad, 1, 1)


def pack_kernel(piece, rows_ref, out_ref):
    out_ref[...] = packed(rows_ref[...])


def partial_kernel(spans, piece, qt_ref, og_ref, rd_ref, kpos_ref, qpos_ref, *refs):
    *piece_refs, mass_ref, vg_ref, peak_ref, sum_ref = refs
    heads, _, tokens = qt_ref.shape
    keys = key_rows(piece_refs, piece, qt_ref.shape[1])
    kpos = jnp.concatenate([kpos_ref[span, :] for span in spans])
    for g in range(0, heads, GROUP):
        cols = slice(g * tokens, (g + GROUP) * tokens)
        scores, value_grads = group_terms(qt_ref, og_ref, keys, kpos, qpos_ref, g)
        row_dots = side_by_side([rd_ref[h] for h in range(g, g + GROUP)])
        vg_ref[:, cols] = (value_grads - row_dots) * QK_HEAD**-0.5
        peak = jnp.max(scores, axis=0, keepdims=True)
        mass = jnp.exp2(scores - peak)
        mass_ref[:, cols] = mass
        peak_ref[:, cols] = peak
        sum_ref[:, cols] = jnp.sum(mass, axis=0, keepdims=True)


def probs_kernel(piece, qt_ref, og_ref, rd_ref, kpos_ref, qpos_ref, *refs):
    *refs, p_ref, ds_ref, far_ref = refs
    *piece_refs, mass0, vg0, peak0, sum0, mass1, vg1, peak1, sum1 = refs
    heads, _, tokens = qt_ref.shape
    width = og_ref.shape[2]
    half = p_ref.shape[0] // 2
    own = mass0.shape[0] // 2
    scale = QK_HEAD**-0.5
    keys = key_rows(piece_refs, piece, qt_ref.shape[1])
    kpos = kpos_ref[half + own :, :]
    for g in range(0, heads, GROUP):
        cols = slice(g * tokens, (g + GROUP) * tokens)
        scores, grads = group_terms(qt_ref, og_ref, keys, kpos, qpos_ref, g)
        last = jnp.max(scores, axis=0, keepdims=True)
        peak = jnp.maximum(jnp.maximum(peak0[:, cols], peak1[:, cols]), last)
        mass = jnp.exp2(scores - peak)
        ratio0, ratio1 = jnp.exp2(peak0[:, cols] - peak), jnp.exp2(peak1[:, cols] - peak)
        total = sum0[:, cols] * ratio0 + sum1[:, cols] * ratio1 + jnp.sum(mass, axis=0, keepdims=True)
        inverse = 1.0 / total
        row_dots = side_by_side([rd_ref[h] for h in range(g, g + GROUP)])
        parts = (
            (slice(0, own), mass0[:own, cols], vg0[:own, cols], inverse * ratio0),
            (slice(half, half + own), mass0[own:, cols], vg0[own:, cols], inverse * ratio0),
            (slice(own, half), mass1[:, cols], vg1[:, cols], inverse * ratio1),
            (slice(half + own, 2 * half), mass, (grads - row_dots) * scale, inverse),
        )
        for rows, part, value_grads, factor in parts:
            weights = part * factor
            p_ref[rows, cols] = weights.astype(bf16)
            ds_ref[rows, cols] = (weights * value_grads).astype(bf16)
    qt = side_by_side([qt_ref[h] for h in range(heads)])
    out_grad = og_ref[...].reshape(heads * tokens, width)
    latent_sums(far_ref, piece, half // 2, ds_ref, p_ref, qt, out_grad, half)


def first_kernel(piece, qt_ref, og_ref, p_ref, ds_ref, near_ref, far_ref):
    heads, _, tokens = qt_ref.shape
    half = p_ref.shape[0] // 2
    qt = side_by_side([qt_ref[h] for h in range(heads)])
    out_grad = og_ref[...].reshape(heads * tokens, og_ref.shape[2])
    latent_sums(near_ref, piece, half // 2, ds_ref, p_ref, qt, out_grad, 0)
    latent_sums(far_ref, piece, half // 2, ds_ref, p_ref, qt, out_grad, half + half // 2)


def last_kernel(piece, qt_ref, og_ref, p_ref, ds_ref, after_ref, near_ref):
    heads, _, tokens = qt_ref.shape
    half = p_ref.shape[0] // 2
    qt = side_by_side([qt_ref[h] for h in range(heads)])
    out_grad = og_ref[...].reshape(heads * tokens, og_ref.shape[2])
    latent_sums(near_ref, piece, half // 2, ds_ref, p_ref, qt, out_grad, half // 2)


def query_kernel(piece, ds_ref, *refs):
    *piece_refs, dq_ref = refs
    heads, kv_width, tokens = dq_ref.shape
    keys = key_rows(piece_refs, piece, kv_width)
    for g in range(0, heads, GROUP):
        grads = dot(keys, ds_ref[:, g * tokens : (g + GROUP) * tokens], 0, 0).astype(bf16)
        for i in range(GROUP):
            dq_ref[g + i] = grads[:, i * tokens : (i + 1) * tokens]


def call(kernel, outs, flops, operands):
    return list(pl.pallas_call(
        kernel,
        in_specs=[VMEM] * len(operands),
        out_specs=[VMEM] * len(outs),
        out_shape=outs,
        compiler_params=pltpu.CompilerParams(vmem_limit_bytes=VMEM_LIMIT),
        cost_estimate=pl.CostEstimate(flops=flops, bytes_accessed=4 << 20, transcendentals=0),
    )(*operands))


def phases_of(device_count):
    bits = device_count.bit_length() - 1
    phases, bit = [[1]], 1
    while bit < bits:
        pair = [1 << bit] if bit + 1 == bits else [1 << bit, 2 << bit, 3 << bit]
        phases.append(pair)
        bit += 1 if len(pair) == 1 else 2
    return phases


def shards(queries, latents, out_grad, outputs, span_map):
    tokens, heads, kv_width = queries.shape
    width = out_grad.shape[2]
    head_size = lax.axis_size("head")
    devices = lax.axis_size("ctx") * head_size
    keys = lax.axis_size("ctx") * tokens
    span_rows = keys // span_map.shape[0]
    ctx, head = lax.axis_index("ctx"), lax.axis_index("head")
    me = ctx * head_size + head
    piece = tokens // head_size
    phases = phases_of(devices)
    around = phases[1][-1:] + phases[1][:-1]
    half_order = [0]
    for masks in [*reversed(phases[2:]), around]:
        half_order = half_order + [m ^ o for m in masks for o in half_order]

    def exchange(value, mask):
        return lax.ppermute(
            value, ("ctx", "head"), [(i, i ^ mask) for i in range(devices)]
        )

    def positions(spans, rows):
        at = rows // span_rows
        mine = at[:, None] == jnp.arange(spans.shape[0], dtype=jnp.int32)[None, :]
        return jnp.sum(jnp.where(mine, spans[None, :], 0), axis=1) * span_rows + rows % span_rows

    qt = queries.transpose(1, 2, 0)
    rows = heads * tokens
    half = keys // 2
    unit = piece if piece % 32 == 0 and kv_width % LANES == LANES // 2 else 0
    columns = LANES if unit else -(-kv_width // LANES) * LANES

    def high(count):
        return count * kv_width // LANES if unit else count

    def kernel(body):
        return functools.partial(body, unit)

    pair_macs = half * rows * (kv_width + width)

    own = lax.dynamic_slice_in_dim(latents, head * piece, piece)
    if unit:
        packed_shape = jax.ShapeDtypeStruct((high(piece), LANES), bf16)
        (own,) = call(kernel(pack_kernel), [packed_shape], 0, [own])
    else:
        own = jnp.pad(own, ((0, 0), (0, columns - kv_width)))
    for masks in reversed(phases[2:]):
        own = jnp.concatenate([own] + [exchange(own, m) for m in masks])
    own, out_grad, outputs, span_map = lax.optimization_barrier((own, out_grad, outputs, span_map))
    near = {m: exchange(own, m) for m in phases[1]}
    near = [near[m] for m in around]
    og = out_grad.transpose(1, 0, 2)
    row_dots = jnp.einsum("ihc,ihc->hi", out_grad, outputs, preferred_element_type=f32)
    row_dots = row_dots.reshape(heads, 1, tokens)
    starts = (me ^ jnp.array(half_order, dtype=jnp.int32)) * piece
    near_rows = (starts[:, None] + jnp.arange(piece, dtype=jnp.int32)[None, :]).reshape(-1)
    near_pos = positions(span_map, near_rows)
    far_pos = positions(span_map, near_rows + jnp.where(head % 2 == 0, piece, -piece))
    query_pos = positions(span_map, ctx * tokens + jnp.arange(tokens, dtype=jnp.int32))[None, :]
    owned = half // (len(around) + 1)
    own, row_dots = lax.optimization_barrier((own, row_dots))
    own_far = exchange(own, 1)

    def in_lanes(pos):
        return jnp.broadcast_to(pos[:, None], (pos.shape[0], LANES))

    key_pos = in_lanes(jnp.concatenate([near_pos, far_pos]))

    def partial_terms(spans, pieces):
        count = sum(span.stop - span.start for span in spans)
        return call(
            kernel(functools.partial(partial_kernel, spans)),
            [
                pltpu.VMEM((count, rows), f32),
                pltpu.VMEM((count, rows), f32),
                pltpu.VMEM((1, rows), f32),
                pltpu.VMEM((1, rows), f32),
            ],
            2 * count * rows * (kv_width + width),
            [qt, og, row_dots, key_pos, query_pos, *pieces],
        )

    terms0 = partial_terms([slice(0, owned), slice(half, half + owned)], [own, own_far])
    near, terms0[2] = lax.optimization_barrier((near, terms0[2]))
    far = [exchange(p, 1) for p in near]
    terms1 = partial_terms([slice(owned, half)], near)
    weights, score_grads, far_a = call(
        kernel(probs_kernel),
        [
            pltpu.VMEM((keys, rows), bf16),
            pltpu.VMEM((keys, rows), bf16),
            jax.ShapeDtypeStruct((high(half // 2), columns), bf16),
        ],
        3 * pair_macs,
        [qt, og, row_dots, key_pos, query_pos, *far, *terms0, *terms1],
    )
    arrived = exchange(far_a, 1)
    near_a, far_b = call(
        kernel(first_kernel),
        [
            jax.ShapeDtypeStruct((high(half // 2), columns), f32),
            jax.ShapeDtypeStruct((high(half // 2), columns), bf16),
        ],
        2 * pair_macs,
        [qt, og, weights, score_grads],
    )
    size = high(owned)
    kept = near_a + arrived.astype(f32)
    leading, after = lax.optimization_barrier((kept[size:].astype(bf16), terms0[2]))
    parts = [exchange(leading, around[0])]
    kept = kept[:size]
    arrived = exchange(far_b, 1)
    (near_b,) = call(
        kernel(last_kernel),
        [jax.ShapeDtypeStruct((high(half // 2), columns), f32)],
        pair_macs,
        [qt, og, weights, score_grads, after],
    )
    if len(around) > 1:
        sent = (near_b + arrived.astype(f32)).astype(bf16)
        parts += [exchange(sent[j * size : (j + 1) * size], m) for j, m in enumerate(around[1:])]
    total = kept + sum(part.astype(f32) for part in parts)
    (query_grads,) = call(
        kernel(query_kernel),
        [jax.ShapeDtypeStruct((heads, kv_width, tokens), bf16)],
        4 * half * rows * kv_width,
        [score_grads, own, *near, own_far, *far],
    )
    total, query_grads = lax.optimization_barrier((total, query_grads))
    for masks in phases[2:]:
        size = total.shape[0] // (len(masks) + 1)
        sent = total.astype(bf16)
        parts = {j: sent[(j + 1) * size : (j + 2) * size] for j in range(len(masks))}
        far_first = [len(masks) - 1, *range(len(masks) - 1)]
        total = total[:size] + sum(exchange(parts[j], masks[j]).astype(f32) for j in far_first)
    latent_grads = unpacked(total, piece, kv_width) if unit else total[:, :kv_width]
    return query_grads.transpose(2, 0, 1), latent_grads


def solution(mesh):
    placed = (
        P("ctx", "head", None),
        P("ctx", None),
        P("ctx", "head", None),
        P("ctx", "head", None),
        P(),
    )
    return jax.shard_map(
        shards,
        mesh=mesh,
        in_specs=placed,
        out_specs=(P("ctx", "head", None), P(("ctx", "head"), None)),
        check_vma=False,
    )
```

```python
import functools

import jax
import jax.numpy as jnp
from jax import lax
from jax.experimental import pallas as pl
from jax.experimental.pallas import tpu as pltpu
from jax.sharding import PartitionSpec as P

QK_HEAD = 192
LARGE_NEGATIVE = -1e30
LOG2_E = 1.4426950408889634
LANES = 128
VMEM_LIMIT = 8 * 1024 * 1024

f32 = jnp.float32
bf16 = jnp.bfloat16
VMEM = pl.BlockSpec(memory_space=pltpu.VMEM)


def dot(a, b, a_dim, b_dim):
    return lax.dot_general(a, b, (((a_dim,), (b_dim,)), ((), ())), preferred_element_type=f32)


def side_by_side(blocks):
    return jnp.concatenate(blocks, axis=1)


def latent_rows(ds_ref, p_ref, qt, out_grad, rows):
    key_term = dot(ds_ref[rows, :], qt, 1, 1)
    value_term = dot(p_ref[rows, :], out_grad, 1, 0)
    width = value_term.shape[1]
    return key_term[:, :width] + value_term, key_term[:, width:]


def packed(rows):
    count, width = rows.shape
    whole = width // LANES * LANES
    blocks = [rows[:, c : c + LANES] for c in range(0, whole, LANES)]
    if whole < width:
        rest = rows[:, whole:]
        blocks.append(jnp.concatenate([rest[: count // 2], rest[count // 2 :]], axis=1))
    return jnp.concatenate(blocks)


def unpacked(blocks, count, width):
    whole = width // LANES
    columns = [blocks[c * count : (c + 1) * count] for c in range(whole)]
    if whole * LANES < width:
        rest = blocks[whole * count :]
        half = LANES // 2
        columns.append(jnp.concatenate([rest[:, :half], rest[:, half:]]))
    return jnp.concatenate(columns, axis=1)


def stored_pieces(out_ref, first, piece, left, right):
    width, rest = left.shape[1], right.shape[1]
    if not piece:
        rows = slice(first, first + left.shape[0])
        out_ref[rows, :width] = left.astype(out_ref.dtype)
        out_ref[rows, width : width + rest] = right.astype(out_ref.dtype)
        unused = out_ref.shape[1] - width - rest
        out_ref[rows, width + rest :] = jnp.zeros((left.shape[0], unused), out_ref.dtype)
        return
    high = piece * (width + rest) // LANES
    for r in range(0, left.shape[0], piece):
        base = (first + r) // piece * high
        for c in range(0, width, LANES):
            at = base + c // LANES * piece
            out_ref[at : at + piece, :] = left[r : r + piece, c : c + LANES].astype(out_ref.dtype)
        middle = r + piece // 2
        folded = jnp.concatenate([right[r:middle], right[middle : r + piece]], axis=1)
        out_ref[base + width // LANES * piece : base + high, :] = folded.astype(out_ref.dtype)


def key_rows(refs, piece, kv_width):
    if not piece:
        return jnp.concatenate([ref[:, :kv_width] for ref in refs])
    high = piece * kv_width // LANES
    return jnp.concatenate(
        [
            unpacked(ref[r : r + high, :], piece, kv_width)
            for ref in refs
            for r in range(0, ref.shape[0], high)
        ]
    )


def latent_sums(out_ref, piece, count, ds_ref, p_ref, qt, out_grad, first):
    step = min(256, count)
    for r in range(0, count, step):
        rows = slice(first + r, first + r + step)
        stored_pieces(out_ref, r, piece, *latent_rows(ds_ref, p_ref, qt, out_grad, rows))


GROUP = 4


def group_terms(qt_ref, og_ref, keys, kpos_ref, qpos_ref, g):
    tokens = qt_ref.shape[2]
    width = og_ref.shape[2]
    qt = side_by_side([qt_ref[h] for h in range(g, g + GROUP)])
    scores = dot(keys, qt, 1, 0)
    allowed = side_by_side([kpos_ref[...]] * GROUP) <= side_by_side([qpos_ref[...]] * GROUP)
    scores = jnp.where(allowed, scores * (QK_HEAD**-0.5 * LOG2_E), LARGE_NEGATIVE)
    out_grad = og_ref[g : g + GROUP].reshape(GROUP * tokens, width)
    return scores, dot(keys[:, :width], out_grad, 1, 1)


def pack_kernel(piece, rows_ref, out_ref):
    out_ref[...] = packed(rows_ref[...])


def partial_kernel(piece, qt_ref, og_ref, rd_ref, kpos_ref, qpos_ref, *refs):
    *piece_refs, mass_ref, vg_ref, peak_ref, sum_ref = refs
    heads, _, tokens = qt_ref.shape
    keys = key_rows(piece_refs, piece, qt_ref.shape[1])
    for g in range(0, heads, GROUP):
        cols = slice(g * tokens, (g + GROUP) * tokens)
        scores, value_grads = group_terms(qt_ref, og_ref, keys, kpos_ref, qpos_ref, g)
        row_dots = side_by_side([rd_ref[h] for h in range(g, g + GROUP)])
        vg_ref[:, cols] = (value_grads - row_dots) * QK_HEAD**-0.5
        peak = jnp.max(scores, axis=0, keepdims=True)
        mass = jnp.exp2(scores - peak)
        mass_ref[:, cols] = mass
        peak_ref[:, cols] = peak
        sum_ref[:, cols] = jnp.sum(mass, axis=0, keepdims=True)


def probs_kernel(piece, qt_ref, og_ref, rd_ref, kpos_ref, qpos_ref, *refs):
    *refs, p_ref, ds_ref, far_ref = refs
    *piece_refs, mass0, vg0, peak0, sum0, mass1, vg1, peak1, sum1 = refs
    heads, _, tokens = qt_ref.shape
    width = og_ref.shape[2]
    half = p_ref.shape[0] // 2
    own = mass0.shape[0] // 2
    scale = QK_HEAD**-0.5
    keys = key_rows(piece_refs, piece, qt_ref.shape[1])
    for g in range(0, heads, GROUP):
        cols = slice(g * tokens, (g + GROUP) * tokens)
        scores, grads = group_terms(qt_ref, og_ref, keys, kpos_ref, qpos_ref, g)
        last = jnp.max(scores, axis=0, keepdims=True)
        peak = jnp.maximum(jnp.maximum(peak0[:, cols], peak1[:, cols]), last)
        mass = jnp.exp2(scores - peak)
        ratio0, ratio1 = jnp.exp2(peak0[:, cols] - peak), jnp.exp2(peak1[:, cols] - peak)
        total = sum0[:, cols] * ratio0 + sum1[:, cols] * ratio1 + jnp.sum(mass, axis=0, keepdims=True)
        inverse = 1.0 / total
        row_dots = side_by_side([rd_ref[h] for h in range(g, g + GROUP)])
        parts = (
            (slice(0, own), mass0[:own, cols], vg0[:own, cols], inverse * ratio0),
            (slice(half, half + own), mass0[own:, cols], vg0[own:, cols], inverse * ratio0),
            (slice(own, half), mass1[:, cols], vg1[:, cols], inverse * ratio1),
            (slice(half + own, 2 * half), mass, (grads - row_dots) * scale, inverse),
        )
        for rows, part, value_grads, factor in parts:
            weights = part * factor
            p_ref[rows, cols] = weights.astype(bf16)
            ds_ref[rows, cols] = (weights * value_grads).astype(bf16)
    qt = side_by_side([qt_ref[h] for h in range(heads)])
    out_grad = og_ref[...].reshape(heads * tokens, width)
    latent_sums(far_ref, piece, half // 2, ds_ref, p_ref, qt, out_grad, half)


def first_kernel(piece, qt_ref, og_ref, p_ref, ds_ref, near_ref, far_ref):
    heads, _, tokens = qt_ref.shape
    half = p_ref.shape[0] // 2
    qt = side_by_side([qt_ref[h] for h in range(heads)])
    out_grad = og_ref[...].reshape(heads * tokens, og_ref.shape[2])
    latent_sums(near_ref, piece, half // 2, ds_ref, p_ref, qt, out_grad, 0)
    latent_sums(far_ref, piece, half // 2, ds_ref, p_ref, qt, out_grad, half + half // 2)


def last_kernel(piece, qt_ref, og_ref, p_ref, ds_ref, after_ref, near_ref):
    heads, _, tokens = qt_ref.shape
    half = p_ref.shape[0] // 2
    qt = side_by_side([qt_ref[h] for h in range(heads)])
    out_grad = og_ref[...].reshape(heads * tokens, og_ref.shape[2])
    latent_sums(near_ref, piece, half // 2, ds_ref, p_ref, qt, out_grad, half // 2)


def query_kernel(piece, ds_ref, *refs):
    *piece_refs, dq_ref = refs
    heads, kv_width, tokens = dq_ref.shape
    keys = key_rows(piece_refs, piece, kv_width)
    for g in range(0, heads, GROUP):
        grads = dot(keys, ds_ref[:, g * tokens : (g + GROUP) * tokens], 0, 0).astype(bf16)
        for i in range(GROUP):
            dq_ref[g + i] = grads[:, i * tokens : (i + 1) * tokens]


def call(kernel, outs, flops, operands):
    return list(pl.pallas_call(
        kernel,
        in_specs=[VMEM] * len(operands),
        out_specs=[VMEM] * len(outs),
        out_shape=outs,
        compiler_params=pltpu.CompilerParams(vmem_limit_bytes=VMEM_LIMIT),
        cost_estimate=pl.CostEstimate(flops=flops, bytes_accessed=4 << 20, transcendentals=0),
    )(*operands))


def phases_of(device_count):
    bits = device_count.bit_length() - 1
    phases, bit = [[1]], 1
    while bit < bits:
        pair = [1 << bit] if bit + 1 == bits else [1 << bit, 2 << bit, 3 << bit]
        phases.append(pair)
        bit += 1 if len(pair) == 1 else 2
    return phases


def shards(queries, latents, out_grad, outputs, span_map):
    tokens, heads, kv_width = queries.shape
    width = out_grad.shape[2]
    head_size = lax.axis_size("head")
    devices = lax.axis_size("ctx") * head_size
    keys = lax.axis_size("ctx") * tokens
    span_rows = keys // span_map.shape[0]
    ctx, head = lax.axis_index("ctx"), lax.axis_index("head")
    me = ctx * head_size + head
    piece = tokens // head_size
    phases = phases_of(devices)
    around = phases[1][-1:] + phases[1][:-1]
    half_order = [0]
    for masks in [*reversed(phases[2:]), around]:
        half_order = half_order + [m ^ o for m in masks for o in half_order]

    def exchange(value, mask):
        return lax.ppermute(
            value, ("ctx", "head"), [(i, i ^ mask) for i in range(devices)]
        )

    def positions(spans, rows):
        at = rows // span_rows
        mine = at[:, None] == jnp.arange(spans.shape[0], dtype=jnp.int32)[None, :]
        return jnp.sum(jnp.where(mine, spans[None, :], 0), axis=1) * span_rows + rows % span_rows

    qt = queries.transpose(1, 2, 0)
    rows = heads * tokens
    half = keys // 2
    unit = piece if piece % 32 == 0 and kv_width % LANES == LANES // 2 else 0
    columns = LANES if unit else -(-kv_width // LANES) * LANES

    def high(count):
        return count * kv_width // LANES if unit else count

    def kernel(body):
        return functools.partial(body, unit)

    pair_macs = half * rows * (kv_width + width)

    own = lax.dynamic_slice_in_dim(latents, head * piece, piece)
    if unit:
        packed_shape = jax.ShapeDtypeStruct((high(piece), LANES), bf16)
        (own,) = call(kernel(pack_kernel), [packed_shape], 0, [own])
    else:
        own = jnp.pad(own, ((0, 0), (0, columns - kv_width)))
    for masks in reversed(phases[2:]):
        own = jnp.concatenate([own] + [exchange(own, m) for m in masks])
    own, out_grad, outputs, span_map = lax.optimization_barrier((own, out_grad, outputs, span_map))
    near = {m: exchange(own, m) for m in (phases[1][1], phases[1][0], phases[1][2])}
    near = [near[m] for m in around]
    og = out_grad.transpose(1, 0, 2)
    row_dots = jnp.einsum("ihc,ihc->hi", out_grad, outputs, preferred_element_type=f32)
    row_dots = row_dots.reshape(heads, 1, tokens)
    starts = (me ^ jnp.array(half_order, dtype=jnp.int32)) * piece
    near_rows = (starts[:, None] + jnp.arange(piece, dtype=jnp.int32)[None, :]).reshape(-1)
    near_pos = positions(span_map, near_rows)
    far_pos = positions(span_map, near_rows + jnp.where(head % 2 == 0, piece, -piece))
    query_pos = positions(span_map, ctx * tokens + jnp.arange(tokens, dtype=jnp.int32))[None, :]
    owned = half // (len(around) + 1)
    own, row_dots = lax.optimization_barrier((own, row_dots))
    own_far = exchange(own, 1)

    def in_lanes(pos):
        return jnp.broadcast_to(pos[:, None], (pos.shape[0], LANES))

    def partial_terms(pos, pieces):
        count = pos.shape[0]
        return call(
            kernel(partial_kernel),
            [
                pltpu.VMEM((count, rows), f32),
                pltpu.VMEM((count, rows), f32),
                pltpu.VMEM((1, rows), f32),
                pltpu.VMEM((1, rows), f32),
            ],
            2 * count * rows * (kv_width + width),
            [qt, og, row_dots, pos, query_pos, *pieces],
        )

    own_lanes, near_lanes, far_lanes = lax.optimization_barrier(
        (
            in_lanes(jnp.concatenate([near_pos[:owned], far_pos[:owned]])),
            in_lanes(near_pos[owned:]),
            in_lanes(far_pos[owned:]),
        )
    )
    terms0 = partial_terms(own_lanes, [own, own_far])
    near, terms0[2] = lax.optimization_barrier((near, terms0[2]))
    far = [exchange(p, 1) for p in near]
    terms1 = partial_terms(near_lanes, near)
    weights, score_grads, far_a = call(
        kernel(probs_kernel),
        [
            pltpu.VMEM((keys, rows), bf16),
            pltpu.VMEM((keys, rows), bf16),
            jax.ShapeDtypeStruct((high(half // 2), columns), bf16),
        ],
        3 * pair_macs,
        [qt, og, row_dots, far_lanes, query_pos, *far, *terms0, *terms1],
    )
    arrived = exchange(far_a, 1)
    near_a, far_b = call(
        kernel(first_kernel),
        [
            jax.ShapeDtypeStruct((high(half // 2), columns), f32),
            jax.ShapeDtypeStruct((high(half // 2), columns), bf16),
        ],
        2 * pair_macs,
        [qt, og, weights, score_grads],
    )
    size = high(owned)
    kept = near_a + arrived.astype(f32)
    leading, after = lax.optimization_barrier((kept[size:].astype(bf16), terms0[2]))
    parts = [exchange(leading, around[0])]
    kept = kept[:size]
    arrived = exchange(far_b, 1)
    (near_b,) = call(
        kernel(last_kernel),
        [jax.ShapeDtypeStruct((high(half // 2), columns), f32)],
        pair_macs,
        [qt, og, weights, score_grads, after],
    )
    if len(around) > 1:
        sent = (near_b + arrived.astype(f32)).astype(bf16)
        parts += [exchange(sent[j * size : (j + 1) * size], m) for j, m in enumerate(around[1:])]
    total = kept + sum(part.astype(f32) for part in parts)
    (query_grads,) = call(
        kernel(query_kernel),
        [jax.ShapeDtypeStruct((heads, kv_width, tokens), bf16)],
        4 * half * rows * kv_width,
        [score_grads, own, *near, own_far, *far],
    )
    total, query_grads = lax.optimization_barrier((total, query_grads))
    for masks in phases[2:]:
        size = total.shape[0] // (len(masks) + 1)
        sent = total.astype(bf16)
        parts = {j: sent[(j + 1) * size : (j + 2) * size] for j in range(len(masks))}
        far_first = [len(masks) - 1, *range(len(masks) - 1)]
        total = total[:size] + sum(exchange(parts[j], masks[j]).astype(f32) for j in far_first)
    latent_grads = unpacked(total, piece, kv_width) if unit else total[:, :kv_width]
    return query_grads.transpose(2, 0, 1), latent_grads


def solution(mesh):
    placed = (
        P("ctx", "head", None),
        P("ctx", None),
        P("ctx", "head", None),
        P("ctx", "head", None),
        P(),
    )
    return jax.shard_map(
        shards,
        mesh=mesh,
        in_specs=placed,
        out_specs=(P("ctx", "head", None), P(("ctx", "head"), None)),
        check_vma=False,
    )
```
